256 devices in a mesh: docs: 2 (over y_hi), ctx: 8 (over z), mp: 16 (over y_lo, x, core).
Axes of the slice: x: 4, y: 4 (y_hi: 2, y_lo: 2; y = y_hi * 2 + y_lo), z: 8, core: 2. Of those that a mesh axis runs over, the one named last changes fastest.
Arguments:
- residual_in: bfloat16 [8192, 5376], P(('docs', 'ctx', 'mp')), parts along dimension 0, may hold values from -15 to 15
- document_start: int32 [8192], P(('docs', 'ctx')), parts along dimension 0, may hold values from 0 to 3584, as said below
- input_gain: float32 [5376], replicated, may hold values from 0.25 to 1.75
- query_weight: bfloat16 [5376, 4096], P(None, 'mp'), may hold values from -0.078125 to 0.078125
- key_weight: bfloat16 [5376, 2048], P(None, 'mp'), may hold values from -0.078125 to 0.078125
- value_weight: bfloat16 [5376, 2048], P(None, 'mp'), may hold values from -0.078125 to 0.078125
- query_gain: float32 [128], replicated, may hold values from 0.6 to 20
- key_gain: float32 [128], replicated, may hold values from 0.6 to 20
- output_weight: bfloat16 [4096, 5376], P('mp'), may hold values from -0.09375 to 0.09375
- post_gain: float32 [5376], replicated, may hold values from 0.25 to 1.75
Outputs:
- residual_out: bfloat16 [8192, 5376], P(('docs', 'ctx', 'mp')), parts along dimension 0
The draws below stay inside these ranges and needn't reach their ends.
There are 2 independent parts, one for each index of `docs`. The reference program is written for one: setup_inputs(seed, part) draws one part's arguments, and reference() takes and returns one part's arrays. A program takes and returns all parts, laid end to end along the dimension named above; an argument that names none is the same for every part. Nothing has to cross between parts.
Inputs may be any that keep to these rules, and one draw needn't show every extreme that they name: `document_start`: each entry is the index of the first token of that token's document; the documents lie end to end, there are 4 of them, one has exactly 3072 tokens, and the last has exactly 512 tokens.
All inputs are finite; a program needn't handle non-finite values.
Results may differ from the reference program's by a relative error of at most 0.014.
The reference program's roundings to bfloat16 on the way count: a program that leaves them out, or rounds other values in their place, can miss the bound.
Values may be sent and summed in bfloat16 or wider, within the bound.
No kernel may reach another device: no remote copies, remote signals or barrier semaphores. Data moves between devices by JAX's collectives and lax.ppermute only.
A program may use at most 64 MiB of HBM per device.

```python
import math
import jax
import jax.numpy as jnp
from jax import lax

D = 5376
HEADS = 32
KV_HEADS = 16
HD = 128
TOKENS = 4096
N_MP = 16


def draw_residual_in(key, part):
    noise_key = jax.random.fold_in(key, 11)
    column_key = jax.random.fold_in(key, 12)
    row_key = jax.random.fold_in(key, 13)
    column_scale = jnp.exp(jax.random.uniform(column_key, (1, D), jnp.float32, math.log(0.2), math.log(2.0)))
    row_scale = jnp.exp(jax.random.uniform(row_key, (TOKENS, 1), jnp.float32, math.log(0.3), math.log(3.0)))
    noise_part = jnp.clip(jax.random.normal(noise_key, (TOKENS, D), jnp.float32), -2.5, 2.5)
    return (noise_part * column_scale * row_scale).astype(jnp.bfloat16)


def draw_document_start(key, part):
    quarter_tokens = TOKENS // 4
    eighth_tokens = TOKENS // 8
    long_length = TOKENS - quarter_tokens
    rest_tokens = quarter_tokens - eighth_tokens
    first_cut = jax.random.randint(jax.random.fold_in(key, 21), (), 1, rest_tokens, dtype=jnp.int32)
    short_lengths = jnp.stack([first_cut, rest_tokens - first_cut])
    long_place = jax.random.randint(jax.random.fold_in(key, 23), (), 0, 3, dtype=jnp.int32)
    slots = jnp.arange(4, dtype=jnp.int32)
    chosen = jnp.clip(slots - (slots > long_place).astype(jnp.int32), 0, 1)
    lengths = jnp.where(slots == long_place, long_length, short_lengths[chosen])
    lengths = jnp.where(slots == 3, eighth_tokens, lengths).astype(jnp.int32)
    starts = jnp.cumsum(lengths) - lengths
    token_index = jnp.arange(TOKENS, dtype=jnp.int32)
    found = jnp.where(starts[None, :] <= token_index[:, None], starts[None, :], 0)
    return jnp.max(found, axis=1).astype(jnp.int32)


def gain_draw(key, which):
    base_key = jax.random.fold_in(key, 1234)
    gain_values = jax.random.uniform(jax.random.fold_in(base_key, which), (HD,), jnp.float32, 0.6, 1.6)
    return gain_values.astype(jnp.float32)


def draw_query_gain(key, part):
    return gain_draw(key, 1)


def draw_key_gain(key, part):
    return gain_draw(key, 2)


def levels(rng, shape, cuts, least, high):
    gain = 1.0
    for dim, blocks in cuts:
        draws = jax.random.uniform(jax.random.fold_in(jax.random.fold_in(rng, 6), dim), (blocks,), jnp.float32, least / len(cuts), high / len(cuts))
        gain = gain * jnp.repeat(jnp.exp(draws), shape[dim] // blocks).reshape((-1,) + (1,) * (len(shape) - 1 - dim))
    return gain


def centred(key, extent, width, bound, split=(), kind=jnp.bfloat16):
    values = width * jax.random.normal(key, extent, jnp.float32)
    if split:
        values = values * levels(key, extent, split, -0.22, 0.18)
    return jnp.clip(values, -bound, bound).astype(kind)


def setup_inputs(seed: int = 0, part: int = 0) -> dict:
    key_of = jax.random.split(jax.random.key(seed), 11)
    part_splits = jax.random.split(jax.random.fold_in(key_of[10], part), 11)
    return {
        "residual_in": draw_residual_in(jax.random.fold_in(jax.random.fold_in(key_of[10], part), 71), part),
        "document_start": draw_document_start(jax.random.fold_in(jax.random.fold_in(key_of[10], part), 71), part),
        "input_gain": jnp.clip(1.0 + 0.15 * jax.random.normal(key_of[2], (D,), jnp.float32), 0.25, 1.75),
        "query_weight": centred(key_of[3], (D, HEADS * HD), D ** -0.5, 0.078125, ((1, 16),)),
        "key_weight": centred(key_of[4], (D, KV_HEADS * HD), D ** -0.5, 0.078125, ((1, 16),)),
        "value_weight": centred(key_of[5], (D, KV_HEADS * HD), D ** -0.5, 0.078125, ((1, 16),)),
        "query_gain": draw_query_gain(jax.random.fold_in(key_of[10], 71), part),
        "key_gain": draw_key_gain(jax.random.fold_in(key_of[10], 71), part),
        "output_weight": centred(key_of[8], (HEADS * HD, D), (HEADS * HD) ** -0.5, 0.09375, ((0, 16),)),
        "post_gain": jnp.clip(1.0 + 0.15 * jax.random.normal(key_of[9], (D,), jnp.float32), 0.25, 1.75),
    }


query_scalar = 168.0
rope_base = 1000000.0
rope_factor = 8.0
epsilon = 1e-06

def make_angles(positions, head_size):
    frequency = rope_base ** (-(jnp.arange(head_size // 2, dtype=jnp.float32) * 2.0 / head_size))
    return (positions.astype(jnp.float32) / rope_factor)[:, None] * frequency[None, :]

def norm_rotate(values, head_gain, angles, head_count):
    tokens_here = values.shape[0]
    head_size = head_gain.shape[0]
    shaped = values.reshape(tokens_here, head_count, head_size)
    scaled = shaped * lax.rsqrt(lax.optimization_barrier(jnp.mean(shaped * shaped, axis=-1, keepdims=True)) + epsilon) * head_gain
    half_size = head_size // 2
    first_half = scaled[..., :half_size]
    second_half = scaled[..., half_size:]
    cosine = jnp.cos(angles)[:, None, :]
    sine_values = jnp.sin(angles)[:, None, :]
    rotated = jnp.concatenate([first_half * cosine - second_half * sine_values, second_half * cosine + first_half * sine_values], axis=-1)
    return rotated.astype(jnp.bfloat16)

def reference(residual_in, document_start, input_gain, query_weight, key_weight, value_weight, query_gain, key_gain, output_weight, post_gain):
    widened = residual_in.astype(jnp.float32)
    normed = (widened * lax.rsqrt(lax.optimization_barrier(jnp.mean(widened * widened, axis=-1, keepdims=True)) + epsilon) * input_gain).astype(jnp.bfloat16)
    query_raw = jnp.dot(normed, query_weight, preferred_element_type=jnp.float32)
    key_raw = jnp.dot(normed, key_weight, preferred_element_type=jnp.float32)
    value_rows = jnp.dot(normed, value_weight, preferred_element_type=jnp.float32).astype(jnp.bfloat16)
    token_index = jnp.arange(TOKENS, dtype=jnp.int32)
    angles = make_angles(token_index - document_start, HD)
    query_rot = norm_rotate(query_raw, query_gain, angles, HEADS)
    key_rot = norm_rotate(key_raw, key_gain, angles, KV_HEADS)
    value_heads = value_rows.reshape(TOKENS, KV_HEADS, HD)
    allowed = (token_index[None, :] >= document_start[:, None]) & (token_index[None, :] <= token_index[:, None])
    group_size = HEADS // KV_HEADS

    def one_head(pair_index):
        query_group = lax.dynamic_slice_in_dim(query_rot, pair_index * group_size, group_size, 1).astype(jnp.float32)
        key_column = lax.dynamic_index_in_dim(key_rot, pair_index, 1, keepdims=False).astype(jnp.float32)
        value_column = lax.dynamic_index_in_dim(value_heads, pair_index, 1, keepdims=False).astype(jnp.float32)
        scores = jnp.einsum('tgd,nd->gtn', query_group, key_column) / math.sqrt(query_scalar)
        scores = jnp.where(allowed[None], scores, -jnp.inf)
        row_max = lax.optimization_barrier(jnp.max(scores, axis=-1, keepdims=True))
        exponent = jnp.exp(scores - row_max)
        rounded = lax.optimization_barrier(exponent.astype(jnp.bfloat16)).astype(jnp.float32)
        numerator = jnp.einsum('gtn,nd->tgd', rounded, value_column)
        denominator = jnp.transpose(lax.optimization_barrier(jnp.sum(exponent, axis=-1)))
        return (numerator / denominator[..., None]).astype(jnp.bfloat16)
    per_head = lax.map(one_head, jnp.arange(KV_HEADS, dtype=jnp.int32))
    attended = jnp.transpose(per_head, (1, 0, 2, 3)).reshape(TOKENS, HEADS * HD)
    group_width = HEADS * HD // N_MP

    def add_group(running, group_index):
        first_column = group_index * group_width
        head_block = lax.dynamic_slice_in_dim(attended, first_column, group_width, 1)
        weight_rows = lax.dynamic_slice_in_dim(output_weight, first_column, group_width, 0)
        group_part = lax.optimization_barrier(jnp.dot(head_block, weight_rows, preferred_element_type=jnp.float32).astype(jnp.bfloat16))
        return (running + group_part.astype(jnp.float32), None)
    summed, unused = lax.scan(add_group, jnp.zeros((TOKENS, D), jnp.float32), jnp.arange(N_MP, dtype=jnp.int32))
    branch = summed * lax.rsqrt(lax.optimization_barrier(jnp.mean(summed * summed, axis=-1, keepdims=True)) + epsilon) * post_gain
    return (widened + branch).astype(jnp.bfloat16)
```

```python
import functools
import math

import jax
import jax.numpy as jnp
from jax import lax
from jax.experimental import pallas as pl
from jax.experimental.pallas import tpu as pltpu
from jax.sharding import PartitionSpec as P

query_scalar = 168.0
rope_base = 1000000.0
rope_factor = 8.0
epsilon = 1e-06

D = 5376
THIRD = D // 3
HD = 128
ROWS = 32
BLOCK = 512
VMEM_LIMIT = 56 * 1024 * 1024

XA, XB, YY, CC = 2, 6, 8, 1
ORDERS = ((XA, XB, YY), (XB, YY, XA), (YY, XA, XB))
BITS = {XA: 1, XB: 2, YY: 4}


def mp_mask(index):
    return (XA if index & 1 else 0) ^ (XB if index & 2 else 0) ^ (YY if index & 4 else 0)


def gathered_order(part):
    first, second, third = (BITS[link] for link in ORDERS[part])
    return [
        (first if k & 1 else 0) | (second if k & 2 else 0) | (third if k & 4 else 0)
        for k in range(8)
    ]


def swap(value, link):
    return lax.ppermute(value, "mp", [(m, m ^ link) for m in range(16)])


def whole(count):
    return [pl.BlockSpec(memory_space=pltpu.VMEM)] * count


def params():
    return pltpu.CompilerParams(vmem_limit_bytes=VMEM_LIMIT)


def shape(rows, columns, dtype=jnp.bfloat16):
    return jax.ShapeDtypeStruct((rows, columns), dtype)


def norm_kernel(x_ref, gain_ref, *outs):
    x = x_ref[...].astype(jnp.float32)
    inverse = lax.rsqrt(jnp.mean(x * x, axis=-1, keepdims=True) + epsilon)
    normed = (x * inverse * gain_ref[...]).astype(jnp.bfloat16)
    for part, out in enumerate(outs):
        out[...] = normed[:, part * THIRD : (part + 1) * THIRD]


def norm_rows(residual, gain):
    return pl.pallas_call(
        norm_kernel,
        out_shape=[shape(ROWS, THIRD)] * 3,
        in_specs=whole(2),
        out_specs=whole(3),
        compiler_params=params(),
        name="norm_rows",
    )(residual, gain.reshape(1, D))


def join_kernel(extra, *refs):
    held, came, outs = refs[0:3], refs[3:6], refs[6:]
    for part in range(3):
        rows = held[part].shape[0]
        outs[part][0:rows] = held[part][...]
        outs[part][rows : 2 * rows] = came[part][...]
        if extra:
            outs[3][part, 0:rows] = held[part][...]
            outs[3][part, rows : 2 * rows] = came[part][...]


def join(held, came, extra):
    rows = held[0].shape[0]
    outs = [shape(2 * rows, THIRD)] * 3
    if extra:
        outs = outs + [jax.ShapeDtypeStruct((3, 2 * rows, THIRD), jnp.bfloat16)]
    return pl.pallas_call(
        functools.partial(join_kernel, extra),
        out_shape=outs,
        in_specs=whole(6),
        out_specs=whole(len(outs)),
        compiler_params=params(),
        name="join_rows",
    )(*held, *came)


def gather_tokens(thirds):
    came = [swap(thirds[p], ORDERS[p][0]) for p in range(3)]
    two = join(thirds, came, False)
    came = [swap(two[p], ORDERS[p][1]) for p in range(3)]
    *four, packed = join(two, came, True)
    late = [swap(four[p], ORDERS[p][2]) for p in range(3)]
    other = swap(packed, CC)
    other_late = [swap(late[p], CC) for p in range(3)]
    return four, late, other, other_late


def rotate(raw, gain, cosine, sine):
    inverse = lax.rsqrt(jnp.mean(raw * raw, axis=-1, keepdims=True) + epsilon)
    scaled = raw * inverse * gain
    turned = pltpu.roll(scaled, HD // 2, 1)
    return (scaled * cosine + turned * sine).astype(jnp.bfloat16)


def project_kernel(weight_count, *refs):
    x_refs = refs[0:10]
    w_refs = refs[10 : 10 + weight_count]
    gain_ref, cos_ref, sin_ref, out_ref, xs, ws, acc, x_sem, w_sem = refs[10 + weight_count :]
    four, late, other, other_late = x_refs[0:3], x_refs[3:6], x_refs[6], x_refs[7:10]
    width = 2 * HD // weight_count
    copies = []
    for part in range(3):
        rows = pl.ds(part * THIRD, THIRD)
        group = []
        for k, w in enumerate(w_refs):
            group.append(
                pltpu.make_async_copy(
                    w.at[rows], ws.at[rows, pl.ds(k * width, width)], w_sem.at[part, k]
                )
            )
        for k, source in enumerate((four[part], late[part], other.at[part], other_late[part])):
            group.append(
                pltpu.make_async_copy(
                    source, xs.at[part, pl.ds(128 * k, 128)], x_sem.at[part, k]
                )
            )
        copies.append(group)
    for group in copies:
        for copy in group:
            copy.start()
    for part in range(3):
        for copy in copies[part]:
            copy.wait()
        product = jnp.dot(
            xs[part],
            ws[part * THIRD : (part + 1) * THIRD],
            preferred_element_type=jnp.float32,
        )
        if part == 0:
            acc[...] = product
        else:
            for k, place in enumerate(gathered_order(part)):
                for core in range(2):
                    to = (core * 8 + place) * ROWS
                    at = (core * 8 + k) * ROWS
                    acc[to : to + ROWS] += product[at : at + ROWS]
    gain = gain_ref[...]
    out_ref[:, 0:HD] = rotate(acc[:, 0:HD], gain, cos_ref[...], sin_ref[...])
    if weight_count == 1:
        out_ref[:, HD : 2 * HD] = rotate(acc[:, HD : 2 * HD], gain, cos_ref[...], sin_ref[...])
    else:
        out_ref[:, HD : 2 * HD] = acc[:, HD : 2 * HD].astype(jnp.bfloat16)


def project(pieces, weights, gain, cosine, sine, name):
    four, late, other, other_late = pieces
    return pl.pallas_call(
        functools.partial(project_kernel, len(weights)),
        out_shape=shape(BLOCK, 2 * HD),
        in_specs=[pl.BlockSpec(memory_space=pl.ANY)] * (10 + len(weights)) + whole(3),
        out_specs=whole(1)[0],
        scratch_shapes=[
            pltpu.VMEM((3, BLOCK, THIRD), jnp.bfloat16),
            pltpu.VMEM((D, 2 * HD), jnp.bfloat16),
            pltpu.VMEM((BLOCK, 2 * HD), jnp.float32),
            pltpu.SemaphoreType.DMA((3, 4)),
            pltpu.SemaphoreType.DMA((3, 2)),
        ],
        compiler_params=params(),
        cost_estimate=pl.CostEstimate(
            flops=2 * BLOCK * D * 2 * HD, bytes_accessed=9000000, transcendentals=0
        ),
        name=name,
    )(*four, *late, other, *other_late, *weights, gain.reshape(1, HD), cosine, sine)


def share_keys(rows):
    def move(value, pairs):
        return lax.ppermute(value, "ctx", pairs)

    forward, backward = rows, rows
    ahead, behind = [], []
    for k in range(3):
        forward = move(forward, [(c, c + 1) for c in range(k, 6)])
        backward = move(backward, [((c - k) % 8, (c - k - 1) % 8) for c in range(3)])
        ahead.append(forward)
        behind.append(backward)
    key_far = move(forward[:, :HD], [(3, 4), (4, 5), (5, 6)])
    value_far = move(backward[:, HD:], [(5, 4), (6, 5), (7, 6)])
    return [rows, *ahead, behind[2], behind[1]], key_far, value_far


NEG = -1e30
TILE = 256


def attend_kernel(
    where_ref,
    q_ref,
    position_ref,
    start_ref,
    offset_ref,
    *refs,
):
    blocks, key_far, value_far = refs[0:6], refs[6], refs[7]
    out_ref, kv, top, total, acc, sem = refs[8:]
    block = where_ref[0]
    live = where_ref[1]
    slots = (0, 1, 2, 3, 5, 6)
    copies = []
    for k, slot in enumerate(slots):
        copies.append((slot, pltpu.make_async_copy(blocks[k], kv.at[slot], sem.at[k])))
    copies.append((4, pltpu.make_async_copy(key_far, kv.at[4, :, pl.ds(0, HD)], sem.at[6])))
    copies.append((4, pltpu.make_async_copy(value_far, kv.at[4, :, pl.ds(HD, HD)], sem.at[7])))
    for slot, copy in copies:
        pl.when(slot < live)(copy.start)
    top[...] = jnp.full(top.shape, NEG, jnp.float32)
    total[...] = jnp.zeros(total.shape, jnp.float32)
    acc[...] = jnp.zeros(acc.shape, jnp.float32)
    for slot, copy in copies:
        pl.when(slot < live)(copy.wait)
    factor = math.log2(math.e) / math.sqrt(query_scalar)

    def step(distance, unused):
        keys = kv[distance, :, 0:HD]
        values = kv[distance, :, HD : 2 * HD]
        first = (block - distance) * BLOCK
        key_index = offset_ref[...] + first
        for tile in range(BLOCK // TILE):
            rows = slice(tile * TILE, (tile + 1) * TILE)
            position = position_ref[rows]
            start = start_ref[rows]
            for head in range(2):
                scores = lax.dot_general(
                    q_ref[rows, head * HD : (head + 1) * HD],
                    keys,
                    (((1,), (1,)), ((), ())),
                    preferred_element_type=jnp.float32,
                )
                pieces = []
                for k in range(BLOCK // HD):
                    index = key_index[:, k * HD : (k + 1) * HD]
                    allowed = (index >= start) & (index <= position)
                    pieces.append(
                        jnp.where(allowed, scores[:, k * HD : (k + 1) * HD] * factor, NEG)
                    )
                best = jnp.maximum(
                    jnp.maximum(pieces[0], pieces[1]), jnp.maximum(pieces[2], pieces[3])
                )
                place = slice(head * BLOCK + tile * TILE, head * BLOCK + (tile + 1) * TILE)
                old = top[place]
                new = jnp.maximum(old, jnp.max(best, axis=-1, keepdims=True))
                fade = jnp.exp2(old - new)
                exps = [jnp.exp2(piece - new) for piece in pieces]
                total[place] = total[place] * fade + (
                    (exps[0] + exps[1]) + (exps[2] + exps[3])
                )
                weights = jnp.concatenate([e.astype(jnp.bfloat16) for e in exps], axis=1)
                acc[place] = acc[place] * fade + jnp.dot(
                    weights, values, preferred_element_type=jnp.float32
                )
                top[place] = new
        return unused

    lax.fori_loop(0, live, step, 0)
    for head in range(2):
        place = slice(head * BLOCK, (head + 1) * BLOCK)
        denominator = jnp.sum(total[place], axis=-1, keepdims=True)
        out_ref[:, head * HD : (head + 1) * HD] = (acc[place] / denominator).astype(jnp.bfloat16)


def attend(where, query, position, start, offset, blocks, key_far, value_far):
    return pl.pallas_call(
        attend_kernel,
        out_shape=shape(BLOCK, 2 * HD),
        in_specs=[pl.BlockSpec(memory_space=pltpu.SMEM)]
        + whole(4)
        + [pl.BlockSpec(memory_space=pl.ANY)] * 8,
        out_specs=whole(1)[0],
        scratch_shapes=[
            pltpu.VMEM((7, BLOCK, 2 * HD), jnp.bfloat16),
            pltpu.VMEM((2 * BLOCK, HD), jnp.float32),
            pltpu.VMEM((2 * BLOCK, HD), jnp.float32),
            pltpu.VMEM((2 * BLOCK, HD), jnp.float32),
            pltpu.SemaphoreType.DMA((8,)),
        ],
        compiler_params=params(),
        name="attend",
    )(where, query, position, start, offset, *blocks, key_far, value_far)


CHUNK = 256


def output_kernel(mine_ref, theirs_ref, w_mine, w_theirs, *outs):
    def groups(weight_columns):
        return jnp.dot(mine_ref[...], w_mine[:, weight_columns], preferred_element_type=jnp.float32).astype(
            jnp.bfloat16
        ).astype(jnp.float32) + jnp.dot(
            theirs_ref[...], w_theirs[:, weight_columns], preferred_element_type=jnp.float32
        ).astype(jnp.bfloat16).astype(jnp.float32)

    for part in range(3):
        bit = BITS[ORDERS[part][0]]
        for chunk in range(THIRD // CHUNK):
            summed = groups(
                slice(part * THIRD + chunk * CHUNK, part * THIRD + (chunk + 1) * CHUNK)
            ).astype(jnp.bfloat16)
            here = slice(chunk * CHUNK, (chunk + 1) * CHUNK)
            counts = [0, 0]
            for place in range(8):
                goes = 1 if place & bit else 0
                at = counts[goes] * ROWS
                counts[goes] += 1
                outs[2 * part + goes][at : at + ROWS, here] = summed[
                    place * ROWS : (place + 1) * ROWS
                ]


def project_out(mine, theirs, w_mine, w_theirs):
    return pl.pallas_call(
        output_kernel,
        out_shape=[shape(128, THIRD)] * 6,
        in_specs=whole(4),
        out_specs=whole(6),
        compiler_params=params(),
        cost_estimate=pl.CostEstimate(
            flops=4 * 256 * 256 * D, bytes_accessed=8500000, transcendentals=0
        ),
        name="project_out",
    )(mine, theirs, w_mine, w_theirs)


def remaining(part, level):
    return sorted(BITS[link] for link in ORDERS[part][level:])


def fold_kernel(level, *refs):
    kept, came, outs = refs[0:3], refs[3:6], refs[6:]
    for part in range(3):
        bits = remaining(part, level)
        goes_bit = bits.index(BITS[ORDERS[part][level]])
        summed = (
            kept[part][...].astype(jnp.float32) + came[part][...].astype(jnp.float32)
        ).astype(jnp.bfloat16)
        counts = [0, 0]
        for k in range(1 << len(bits)):
            goes = (k >> goes_bit) & 1
            at = counts[goes] * ROWS
            counts[goes] += 1
            outs[2 * part + goes][at : at + ROWS] = summed[k * ROWS : (k + 1) * ROWS]


def fold(kept, came, level):
    rows = kept[0].shape[0] // 2
    return pl.pallas_call(
        functools.partial(fold_kernel, level),
        out_shape=[shape(rows, THIRD)] * 6,
        in_specs=whole(6),
        out_specs=whole(6),
        compiler_params=params(),
        name="fold_rows",
    )(*kept, *came)


def finish_kernel(residual_ref, gain_ref, *refs):
    kept, came, out = refs[0:3], refs[3:6], refs[6]
    sums = []
    square = jnp.zeros((ROWS, 1), jnp.float32)
    for part in range(3):
        summed = kept[part][...].astype(jnp.float32) + came[part][...].astype(jnp.float32)
        sums.append(summed)
        square = square + jnp.sum(summed * summed, axis=-1, keepdims=True)
    inverse = lax.rsqrt(square / D + epsilon)
    for part in range(3):
        here = slice(part * THIRD, (part + 1) * THIRD)
        out[:, here] = (
            residual_ref[:, here].astype(jnp.float32) + sums[part] * inverse * gain_ref[:, here]
        ).astype(jnp.bfloat16)


def finish(residual, gain, kept, came):
    return pl.pallas_call(
        finish_kernel,
        out_shape=shape(ROWS, D),
        in_specs=whole(8),
        out_specs=whole(1)[0],
        compiler_params=params(),
        name="finish",
    )(residual, gain.reshape(1, D), *kept, *came)


def reduce_tokens(halves):
    kept, goes = halves[0::2], halves[1::2]
    for level in range(3):
        came = [swap(goes[p], ORDERS[p][level]) for p in range(3)]
        if level == 2:
            return kept, came
        halves = fold(kept, came, level + 1)
        kept, goes = halves[0::2], halves[1::2]


def body(
    residual_in,
    document_start,
    input_gain,
    query_weight,
    key_weight,
    value_weight,
    query_gain,
    key_gain,
    output_weight,
    post_gain,
):
    thirds = norm_rows(residual_in, input_gain)
    pieces = gather_tokens(thirds)

    block = lax.axis_index("ctx")
    mine = lax.axis_index("mp")
    masks = jnp.array([mp_mask(k & 7) ^ (k >> 3) for k in range(16)], jnp.int32)
    owners = mine ^ masks
    inside = (owners[:, None] * ROWS + jnp.arange(ROWS, dtype=jnp.int32)[None, :]).reshape(BLOCK)
    position = block * BLOCK + inside
    start = document_start.reshape(16, ROWS)[owners].reshape(BLOCK)
    frequency = rope_base ** (-(jnp.arange(HD // 2, dtype=jnp.float32) * 2.0 / HD))
    angles = ((position - start).astype(jnp.float32) / rope_factor)[:, None] * frequency[None, :]
    cosine = jnp.cos(angles)
    sine = jnp.sin(angles)
    cosine = jnp.concatenate([cosine, cosine], axis=1)
    sine = jnp.concatenate([-sine, sine], axis=1)
    live = block - jnp.min(document_start) // BLOCK + 1
    where = jnp.stack([block, live]).astype(jnp.int32)
    position_wide = jnp.broadcast_to(position[:, None], (BLOCK, HD))
    start_wide = jnp.broadcast_to(start[:, None], (BLOCK, HD))

    w_theirs = swap(output_weight, CC)
    rows = project(pieces, [key_weight, value_weight], key_gain, cosine, sine, "project_kv")
    query = project(pieces, [query_weight], query_gain, cosine, sine, "project_q")
    blocks, key_far, value_far = share_keys(rows)
    attended = attend(
        where, query, position_wide, start_wide, inside[None, :], blocks, key_far, value_far
    )
    theirs = swap(attended[256:], CC)
    halves = project_out(attended[:256], theirs, output_weight, w_theirs)
    kept, came = reduce_tokens(halves)
    return finish(residual_in, post_gain, kept, came)


def solution(mesh):
    return jax.shard_map(
        body,
        mesh=mesh,
        in_specs=(
            P(("docs", "ctx", "mp"), None),
            P(("docs", "ctx")),
            P(),
            P(None, "mp"),
            P(None, "mp"),
            P(None, "mp"),
            P(),
            P(),
            P("mp", None),
            P(),
        ),
        out_specs=P(("docs", "ctx", "mp"), None),
        check_vma=False,
    )
```

```python
import functools
import math

import jax
import jax.numpy as jnp
from jax import lax
from jax.experimental import pallas as pl
from jax.experimental.pallas import tpu as pltpu
from jax.sharding import PartitionSpec as P

query_scalar = 168.0
rope_base = 1000000.0
rope_factor = 8.0
epsilon = 1e-06

D = 5376
THIRD = D // 3
HD = 128
ROWS = 32
BLOCK = 512

XA, XB, YY, CC = 2, 6, 8, 1
ORDERS = ((XA, XB, YY), (XB, YY, XA), (YY, XA, XB))
BITS = {XA: 1, XB: 2, YY: 4}


def mp_mask(index):
    return (XA if index & 1 else 0) ^ (XB if index & 2 else 0) ^ (YY if index & 4 else 0)


def gathered_order(part):
    first, second, third = (BITS[link] for link in ORDERS[part])
    return [
        (first if k & 1 else 0) | (second if k & 2 else 0) | (third if k & 4 else 0)
        for k in range(8)
    ]


def swap(value, link):
    return lax.ppermute(value, "mp", [(m, m ^ link) for m in range(16)])


def whole(count):
    return [pl.BlockSpec(memory_space=pltpu.VMEM)] * count


def params(mebibytes):
    return pltpu.CompilerParams(vmem_limit_bytes=mebibytes * 1024 * 1024)


def shape(rows, columns, dtype=jnp.bfloat16):
    return jax.ShapeDtypeStruct((rows, columns), dtype)


def norm_kernel(x_ref, gain_ref, *outs):
    square = jnp.zeros((ROWS, HD), jnp.float32)
    for k in range(D // HD):
        x = x_ref[:, k * HD : (k + 1) * HD].astype(jnp.float32)
        square = square + x * x
    inverse = lax.rsqrt(jnp.sum(square, axis=-1, keepdims=True) / D + epsilon)
    for part, out in enumerate(outs):
        for k in range(THIRD // HD):
            at = part * (THIRD // HD) + k
            x = x_ref[:, at * HD : (at + 1) * HD].astype(jnp.float32)
            out[:, k * HD : (k + 1) * HD] = (x * inverse * gain_ref[at : at + 1]).astype(
                jnp.bfloat16
            )


def norm_rows(residual, gain):
    return pl.pallas_call(
        norm_kernel,
        out_shape=[shape(ROWS, THIRD)] * 3,
        in_specs=whole(2),
        out_specs=whole(3),
        compiler_params=params(4),
        name="norm_rows",
    )(residual, gain.reshape(D // HD, HD))


def join_kernel(extra, *refs):
    held, came, outs = refs[0:3], refs[3:6], refs[6:]
    for part in range(3):
        rows = held[part].shape[0]
        outs[part][0:rows] = held[part][...]
        outs[part][rows : 2 * rows] = came[part][...]
        if extra:
            outs[3][part, 0:rows] = held[part][...]
            outs[3][part, rows : 2 * rows] = came[part][...]


def join(held, came, extra):
    rows = held[0].shape[0]
    outs = [shape(2 * rows, THIRD)] * 3
    if extra:
        outs = outs + [jax.ShapeDtypeStruct((3, 2 * rows, THIRD), jnp.bfloat16)]
    return pl.pallas_call(
        functools.partial(join_kernel, extra),
        out_shape=outs,
        in_specs=whole(6),
        out_specs=whole(len(outs)),
        compiler_params=params(10),
        name="join_rows",
    )(*held, *came)


def gather_tokens(thirds, tables):
    came = [swap(thirds[p], ORDERS[p][0]) for p in range(3)]
    two = join(thirds, came, False)
    came = [swap(two[p], ORDERS[p][1]) for p in range(3)]
    *four, packed = join(two, came, True)
    late = [swap(four[p], ORDERS[p][2]) for p in range(3)]
    other = swap(packed, CC)
    *late, cosine, sine, where, position, start, offset = lax.optimization_barrier(
        (*late, *tables)
    )
    other_late = [swap(late[p], CC) for p in range(3)]
    return (four, late, other, other_late), cosine, sine, where, position, start, offset


def rotate(raw, gain, cosine, sine):
    inverse = lax.rsqrt(jnp.mean(raw * raw, axis=-1, keepdims=True) + epsilon)
    scaled = raw * inverse * gain
    turned = pltpu.roll(scaled, HD // 2, 1)
    return (scaled * cosine + turned * sine).astype(jnp.bfloat16)


def project_kernel(weight_count, *refs):
    x_refs = refs[0:10]
    w_refs = refs[10 : 10 + weight_count]
    gain_ref, cos_ref, sin_ref, out_ref = refs[10 + weight_count :]
    four, late, other, other_late = x_refs[0:3], x_refs[3:6], x_refs[6], x_refs[7:10]
    total = None
    for part in range(3):
        order = gathered_order(part)
        rows = []
        for core in range(2):
            for place in range(8):
                k = order.index(place)
                at = (k % 4) * ROWS
                if core == 0:
                    rows.append((four if k < 4 else late)[part][at : at + ROWS])
                elif k < 4:
                    rows.append(other[part, at : at + ROWS])
                else:
                    rows.append(other_late[part][at : at + ROWS])
        weights = [w[part * THIRD : (part + 1) * THIRD] for w in w_refs]
        product = jnp.dot(
            jnp.concatenate(rows, axis=0),
            jnp.concatenate(weights, axis=1) if weight_count == 2 else weights[0],
            preferred_element_type=jnp.float32,
        )
        total = product if part == 0 else total + product
    gain = gain_ref[...]
    out_ref[:, 0:HD] = rotate(total[:, 0:HD], gain, cos_ref[...], sin_ref[...])
    if weight_count == 1:
        out_ref[:, HD : 2 * HD] = rotate(total[:, HD : 2 * HD], gain, cos_ref[...], sin_ref[...])
    else:
        out_ref[:, HD : 2 * HD] = total[:, HD : 2 * HD].astype(jnp.bfloat16)


def project(pieces, weights, gain, cosine, sine, name):
    four, late, other, other_late = pieces
    return pl.pallas_call(
        functools.partial(project_kernel, len(weights)),
        out_shape=shape(BLOCK, 2 * HD),
        in_specs=whole(13 + len(weights)),
        out_specs=whole(1)[0],
        compiler_params=params(18),
        cost_estimate=pl.CostEstimate(
            flops=2 * BLOCK * D * 2 * HD, bytes_accessed=9000000, transcendentals=0
        ),
        name=name,
    )(*four, *late, other, *other_late, *weights, gain.reshape(1, HD), cosine, sine)


NEG = -1e30
TILE = 256


def move(value, pairs):
    return lax.ppermute(value, "ctx", pairs)


def attend_kernel(distances, joint, first, last, *refs):
    where_ref, q_ref, position_ref, start_ref, offset_ref = refs[0:5]
    refs = refs[5:]
    blocks, refs = refs[: len(joint)], refs[len(joint) :]
    if not first:
        old_state, refs = refs[0:3], refs[3:]
    if last:
        out_ref, state = refs[0], refs[1:4]
    else:
        state = refs[0:3]
    top, total, acc = state
    block = where_ref[0]
    live = where_ref[1]
    rows_here = q_ref.shape[0]
    factor = math.log2(math.e) / math.sqrt(query_scalar)

    def step(distance, keys_ref, values_ref, source):
        opening = source is None
        keys = keys_ref[...]
        values = values_ref[...]
        key_index = offset_ref[...] + (block - distance) * BLOCK
        for tile in range(rows_here // TILE):
            rows = slice(tile * TILE, (tile + 1) * TILE)
            position = position_ref[rows]
            start = start_ref[rows]
            for head in range(2):
                scores = lax.dot_general(
                    q_ref[rows, head * HD : (head + 1) * HD],
                    keys,
                    (((1,), (1,)), ((), ())),
                    preferred_element_type=jnp.float32,
                )
                pieces = []
                for k in range(BLOCK // HD):
                    index = key_index[:, k * HD : (k + 1) * HD]
                    allowed = index >= start
                    if distance == 0:
                        allowed = allowed & (index <= position)
                    pieces.append(
                        jnp.where(allowed, scores[:, k * HD : (k + 1) * HD] * factor, NEG)
                    )
                best = jnp.maximum(
                    jnp.maximum(pieces[0], pieces[1]), jnp.maximum(pieces[2], pieces[3])
                )
                best = jnp.max(best, axis=-1, keepdims=True)
                if opening:
                    new = jnp.broadcast_to(best, (TILE, HD))
                else:
                    old = source[0][head, rows]
                    new = jnp.maximum(old, best)
                exps = [jnp.exp2(piece - new) for piece in pieces]
                sums = (exps[0] + exps[1]) + (exps[2] + exps[3])
                weights = jnp.concatenate([e.astype(jnp.bfloat16) for e in exps], axis=1)
                product = jnp.dot(weights, values, preferred_element_type=jnp.float32)
                if not opening:
                    fade = jnp.exp2(old - new)
                    sums = source[1][head, rows] * fade + sums
                    product = source[2][head, rows] * fade + product
                total[head, rows] = sums
                acc[head, rows] = product
                top[head, rows] = new

    def keep():
        for new_ref, old_ref in zip(state, old_state):
            new_ref[...] = old_ref[...]

    source = None if first else old_state
    k = 0
    for distance, whole_block in zip(distances, joint):
        if whole_block == 2:
            continue
        if whole_block:
            keys_ref = blocks[k].at[:, pl.ds(0, HD)]
            values_ref = blocks[k].at[:, pl.ds(HD, HD)]
            k += 1
        else:
            keys_ref, values_ref = blocks[k], blocks[k + 1]
            k += 2
        if distance == 0:
            step(0, keys_ref, values_ref, None)
        else:
            pl.when(distance < live)(
                functools.partial(step, distance, keys_ref, values_ref, source)
            )
            if source is not state:
                pl.when(distance >= live)(keep)
        source = state
    if last:
        for head in range(2):
            denominator = jnp.sum(total[head], axis=-1, keepdims=True)
            out_ref[:, head * HD : (head + 1) * HD] = (acc[head] / denominator).astype(
                jnp.bfloat16
            )


def attend(tables, query, distances, joint, blocks, state, last, half=None):
    where, position, start, offset = tables
    first = state is None
    state = () if first else tuple(state)
    rows_here = BLOCK // 2 if last else BLOCK
    state_shape = jax.ShapeDtypeStruct((2, rows_here, HD), jnp.float32)
    if last:
        out_shape, out_specs = shape(rows_here, 2 * HD), whole(1)[0]
        scratch = [pltpu.VMEM((2, rows_here, HD), jnp.float32)] * 3
        row_specs = [
            pl.BlockSpec((rows_here, 2 * HD), lambda k: (half, 0)),
            pl.BlockSpec((rows_here, HD), lambda k: (half, 0)),
            pl.BlockSpec((rows_here, HD), lambda k: (half, 0)),
        ]
        state_specs = [pl.BlockSpec((2, rows_here, HD), lambda k: (0, half, 0))] * 3
    else:
        out_shape, out_specs = [state_shape] * 3, whole(3)
        scratch = []
        row_specs = whole(3)
        state_specs = whole(3)
    return pl.pallas_call(
        functools.partial(attend_kernel, distances, joint, first, last),
        out_shape=out_shape,
        grid=(1,) if last else (),
        in_specs=[pl.BlockSpec(memory_space=pltpu.SMEM)]
        + row_specs
        + whole(1 + len(blocks))
        + (state_specs if state else []),
        out_specs=out_specs,
        scratch_shapes=scratch,
        compiler_params=params(12),
        cost_estimate=pl.CostEstimate(
            flops=800000000 * len(distances), bytes_accessed=3000000, transcendentals=1000000
        ),
        name="attend",
    )(where, query, position, start, offset, *blocks, *state)


def share_and_attend(rows, make_query, tables):
    tie = lax.optimization_barrier
    forward, backward = rows, rows

    def onward(k, forward, backward):
        return (
            move(forward, [(c, c + 1) for c in range(k, 6)]),
            move(backward, [((c - k) % 8, (c - k - 1) % 8) for c in range(3)]),
        )

    one, back_one = onward(0, rows, rows)
    query = make_query()
    state = attend(tables, query, (0,), (1,), [rows], None, False)
    one, back_one, state = tie((one, back_one, state))
    two, back_two = onward(1, one, back_one)
    state = attend(tables, query, (1,), (1,), [one], state, False)
    two, back_two, state = tie((two, back_two, state))
    three, back_three = onward(2, two, back_two)
    state = attend(tables, query, (2, 6), (1, 1), [two, back_two], state, False)
    three, back_three, state = tie((three, back_three, state))
    key_far = move(three[:, :HD], [(3, 4), (4, 5), (5, 6)])
    value_far = move(back_three[:, HD:], [(5, 4), (6, 5), (7, 6)])
    state = attend(tables, query, (3, 5), (1, 1), [three, back_three], state, False)
    key_far, value_far, state = tie((key_far, value_far, state))
    goes = attend(tables, query, (4,), (0, 2), [key_far, value_far], state, True, 1)
    stays = attend(tables, query, (4,), (0, 2), [key_far, value_far], state, True, 0)
    return stays, swap(goes, CC)


CHUNK = 256


def output_kernel(mine_ref, theirs_ref, w_mine, w_theirs, *outs):
    def groups(weight_columns):
        return jnp.dot(mine_ref[...], w_mine[:, weight_columns], preferred_element_type=jnp.float32).astype(
            jnp.bfloat16
        ).astype(jnp.float32) + jnp.dot(
            theirs_ref[...], w_theirs[:, weight_columns], preferred_element_type=jnp.float32
        ).astype(jnp.bfloat16).astype(jnp.float32)

    for part in range(3):
        bit = BITS[ORDERS[part][0]]
        for chunk in range(THIRD // CHUNK):
            summed = groups(
                slice(part * THIRD + chunk * CHUNK, part * THIRD + (chunk + 1) * CHUNK)
            ).astype(jnp.bfloat16)
            here = slice(chunk * CHUNK, (chunk + 1) * CHUNK)
            counts = [0, 0]
            for place in range(8):
                goes = 1 if place & bit else 0
                at = counts[goes] * ROWS
                counts[goes] += 1
                outs[2 * part + goes][at : at + ROWS, here] = summed[
                    place * ROWS : (place + 1) * ROWS
                ]


def project_out(mine, theirs, w_mine, w_theirs):
    return pl.pallas_call(
        output_kernel,
        out_shape=[shape(128, THIRD)] * 6,
        in_specs=whole(4),
        out_specs=whole(6),
        compiler_params=params(24),
        cost_estimate=pl.CostEstimate(
            flops=4 * 256 * 256 * D, bytes_accessed=8500000, transcendentals=0
        ),
        name="project_out",
    )(mine, theirs, w_mine, w_theirs)


def remaining(part, level):
    return sorted(BITS[link] for link in ORDERS[part][level:])


def fold_kernel(level, *refs):
    kept, came, outs = refs[0:3], refs[3:6], refs[6:]
    for part in range(3):
        bits = remaining(part, level)
        goes_bit = bits.index(BITS[ORDERS[part][level]])
        summed = (
            kept[part][...].astype(jnp.float32) + came[part][...].astype(jnp.float32)
        ).astype(jnp.bfloat16)
        counts = [0, 0]
        for k in range(1 << len(bits)):
            goes = (k >> goes_bit) & 1
            at = counts[goes] * ROWS
            counts[goes] += 1
            outs[2 * part + goes][at : at + ROWS] = summed[k * ROWS : (k + 1) * ROWS]


def fold(kept, came, level):
    rows = kept[0].shape[0] // 2
    return pl.pallas_call(
        functools.partial(fold_kernel, level),
        out_shape=[shape(rows, THIRD)] * 6,
        in_specs=whole(6),
        out_specs=whole(6),
        compiler_params=params(12),
        name="fold_rows",
    )(*kept, *came)


def finish_kernel(residual_ref, gain_ref, *refs):
    kept, came, out, sums = refs[0:3], refs[3:6], refs[6], refs[7]
    square = jnp.zeros((ROWS, HD), jnp.float32)
    for part in range(3):
        for k in range(THIRD // HD):
            here = slice(k * HD, (k + 1) * HD)
            summed = kept[part][:, here].astype(jnp.float32) + came[part][:, here].astype(
                jnp.float32
            )
            at = part * THIRD + k * HD
            sums[:, at : at + HD] = summed
            square = square + summed * summed
    inverse = lax.rsqrt(jnp.sum(square, axis=-1, keepdims=True) / D + epsilon)
    for k in range(D // HD):
        here = slice(k * HD, (k + 1) * HD)
        out[:, here] = (
            residual_ref[:, here].astype(jnp.float32)
            + sums[:, here] * inverse * gain_ref[k : k + 1]
        ).astype(jnp.bfloat16)


def finish(residual, gain, kept, came):
    return pl.pallas_call(
        finish_kernel,
        out_shape=shape(ROWS, D),
        in_specs=whole(8),
        out_specs=whole(1)[0],
        scratch_shapes=[pltpu.VMEM((ROWS, D), jnp.float32)],
        compiler_params=params(6),
        name="finish",
    )(residual, gain.reshape(D // HD, HD), *kept, *came)


def reduce_tokens(halves):
    kept, goes = halves[0::2], halves[1::2]
    for level in range(3):
        came = [swap(goes[p], ORDERS[p][level]) for p in range(3)]
        if level == 2:
            return kept, came
        halves = fold(kept, came, level + 1)
        kept, goes = halves[0::2], halves[1::2]


def body(
    residual_in,
    document_start,
    input_gain,
    query_weight,
    key_weight,
    value_weight,
    query_gain,
    key_gain,
    output_weight,
    post_gain,
):
    thirds = norm_rows(residual_in, input_gain)

    block = lax.axis_index("ctx")
    mine = lax.axis_index("mp")
    masks = jnp.array([mp_mask(k & 7) ^ (k >> 3) for k in range(16)], jnp.int32)
    owners = mine ^ masks
    inside = (owners[:, None] * ROWS + jnp.arange(ROWS, dtype=jnp.int32)[None, :]).reshape(BLOCK)
    position = block * BLOCK + inside
    start = document_start.reshape(16, ROWS)[owners].reshape(BLOCK)
    frequency = rope_base ** (-(jnp.arange(HD // 2, dtype=jnp.float32) * 2.0 / HD))
    angles = ((position - start).astype(jnp.float32) / rope_factor)[:, None] * frequency[None, :]
    cosine = jnp.cos(angles)
    sine = jnp.sin(angles)
    cosine = jnp.concatenate([cosine, cosine], axis=1)
    sine = jnp.concatenate([-sine, sine], axis=1)
    live = block - jnp.min(document_start) // BLOCK + 1
    where = jnp.stack([block, live]).astype(jnp.int32)
    position_wide = jnp.broadcast_to(position[:, None], (BLOCK, HD))
    start_wide = jnp.broadcast_to(start[:, None], (BLOCK, HD))

    pieces, cosine, sine, where, position_wide, start_wide, offset = gather_tokens(
        thirds, (cosine, sine, where, position_wide, start_wide, inside[None, :])
    )
    w_theirs = swap(output_weight, CC)
    tables = (where, position_wide, start_wide, offset)
    rows = project(pieces, [key_weight, value_weight], key_gain, cosine, sine, "project_kv")
    mine, theirs = share_and_attend(
        rows,
        lambda: project(pieces, [query_weight], query_gain, cosine, sine, "project_q"),
        tables,
    )
    halves = project_out(mine, theirs, output_weight, w_theirs)
    kept, came = reduce_tokens(halves)
    return finish(residual_in, post_gain, kept, came)


def solution(mesh):
    return jax.shard_map(
        body,
        mesh=mesh,
        in_specs=(
            P(("docs", "ctx", "mp"), None),
            P(("docs", "ctx")),
            P(),
            P(None, "mp"),
            P(None, "mp"),
            P(None, "mp"),
            P(),
            P(),
            P("mp", None),
            P(),
        ),
        out_specs=P(("docs", "ctx", "mp"), None),
        check_vma=False,
    )
```

```python
import functools
import math

import jax
import jax.numpy as jnp
import numpy as np
from jax import lax
from jax.experimental import pallas as pl
from jax.experimental.pallas import tpu as pltpu
from jax.sharding import PartitionSpec as P

query_scalar = 168.0
rope_base = 1000000.0
rope_factor = 8.0
epsilon = 1e-06

D = 5376
THIRD = D // 3
HD = 128
ROWS = 32
BLOCK = 512

XA, XB, YY, CC = 2, 6, 8, 1
ORDERS = ((XA, XB, YY), (XB, YY, XA), (YY, XA, XB))
BITS = {XA: 1, XB: 2, YY: 4}


def mp_mask(index):
    return (XA if index & 1 else 0) ^ (XB if index & 2 else 0) ^ (YY if index & 4 else 0)


def gathered_order(part):
    first, second, third = (BITS[link] for link in ORDERS[part])
    return [
        (first if k & 1 else 0) | (second if k & 2 else 0) | (third if k & 4 else 0)
        for k in range(8)
    ]


def swap(value, link):
    return lax.ppermute(value, "mp", [(m, m ^ link) for m in range(16)])


def swap_y_both_ways(value):
    return lax.ppermute(
        value,
        ("docs", "mp"),
        [(d * 16 + m, (d ^ (m & 1)) * 16 + (m ^ YY)) for d in range(2) for m in range(16)],
    )


def whole(count):
    return [pl.BlockSpec(memory_space=pltpu.VMEM)] * count


def params(mebibytes):
    return pltpu.CompilerParams(vmem_limit_bytes=mebibytes * 1024 * 1024)


def shape(rows, columns, dtype=jnp.bfloat16):
    return jax.ShapeDtypeStruct((rows, columns), dtype)


def norm_kernel(x_ref, gain_ref, *outs):
    square = jnp.zeros((ROWS, HD), jnp.float32)
    for k in range(D // HD):
        x = x_ref[:, k * HD : (k + 1) * HD].astype(jnp.float32)
        square = square + x * x
    inverse = lax.rsqrt(jnp.sum(square, axis=-1, keepdims=True) / D + epsilon)
    for part, out in enumerate(outs):
        for k in range(THIRD // HD):
            at = part * (THIRD // HD) + k
            x = x_ref[:, at * HD : (at + 1) * HD].astype(jnp.float32)
            out[:, k * HD : (k + 1) * HD] = (x * inverse * gain_ref[at : at + 1]).astype(
                jnp.bfloat16
            )


def norm_rows(residual, gain):
    return pl.pallas_call(
        norm_kernel,
        out_shape=[shape(ROWS, THIRD)] * 3,
        in_specs=whole(2),
        out_specs=whole(3),
        compiler_params=params(4),
        name="norm_rows",
    )(residual, gain.reshape(D // HD, HD))


def tables_kernel(
    starts_ref, first_ref, frequency_ref, cos_ref, sin_ref, position_ref, start_ref, offset_ref, where_ref, natural
):
    mine = lax.axis_index("mp")
    block = lax.axis_index("ctx")
    row = lax.broadcasted_iota(jnp.int32, (HD, HD), 0)
    lane = lax.broadcasted_iota(jnp.int32, (HD, HD), 1)
    for k in range(BLOCK // HD):
        spread = jnp.broadcast_to(starts_ref[k : k + 1].astype(jnp.float32), (HD, HD))
        column = jnp.sum(jnp.where(row == lane, spread, 0.0), axis=-1, keepdims=True)
        natural[k * HD : (k + 1) * HD] = jnp.broadcast_to(column, (HD, HD)).astype(jnp.int32)
    inner = lax.broadcasted_iota(jnp.int32, (ROWS, HD), 0)
    along = lax.broadcasted_iota(jnp.int32, (1, BLOCK), 1)
    offset = along
    sign = jnp.where(
        lax.broadcasted_iota(jnp.int32, (ROWS, HD), 1) < HD // 2, -1.0, 1.0
    )
    for k in range(16):
        owner = mine ^ (mp_mask(k & 7) ^ (k >> 3))
        here = slice(k * ROWS, (k + 1) * ROWS)
        start = natural[pl.ds(pl.multiple_of(owner * ROWS, ROWS), ROWS)]
        position = inner + (block * BLOCK + owner * ROWS)
        start_ref[here] = start
        position_ref[here] = position
        angles = ((position - start).astype(jnp.float32) / rope_factor) * frequency_ref[...]
        cos_ref[here] = jnp.cos(angles)
        sin_ref[here] = jnp.sin(angles) * sign
        inside = (along >= k * ROWS) & (along < (k + 1) * ROWS)
        offset = jnp.where(inside, along + (owner - k) * ROWS, offset)
    offset_ref[...] = offset
    where_ref[0] = block
    where_ref[1] = block - (first_ref[0] >> 9) + 1


def make_tables(document_start):
    frequency = np.float32(rope_base) ** (
        -(np.arange(HD // 2, dtype=np.float32) * np.float32(2.0) / np.float32(HD))
    )
    frequency = jnp.asarray(np.concatenate([frequency, frequency])[None, :], jnp.float32)
    wide = lambda kind: jax.ShapeDtypeStruct((BLOCK, HD), kind)
    return pl.pallas_call(
        tables_kernel,
        out_shape=[
            wide(jnp.float32),
            wide(jnp.float32),
            wide(jnp.int32),
            wide(jnp.int32),
            jax.ShapeDtypeStruct((1, BLOCK), jnp.int32),
            jax.ShapeDtypeStruct((2,), jnp.int32),
        ],
        in_specs=[
            pl.BlockSpec(memory_space=pltpu.VMEM),
            pl.BlockSpec(memory_space=pltpu.SMEM),
            pl.BlockSpec(memory_space=pltpu.VMEM),
        ],
        out_specs=whole(5) + [pl.BlockSpec(memory_space=pltpu.SMEM)],
        scratch_shapes=[pltpu.VMEM((BLOCK, HD), jnp.int32)],
        compiler_params=params(4),
        cost_estimate=pl.CostEstimate(
            flops=4000000, bytes_accessed=1000000, transcendentals=131072
        ),
        name="tables",
    )(document_start.reshape(BLOCK // HD, HD), document_start, frequency)


def join_kernel(extra, *refs):
    held, came, outs = refs[0:3], refs[3:6], refs[6:]
    for part in range(3):
        rows = held[part].shape[0]
        outs[part][0:rows] = held[part][...]
        outs[part][rows : 2 * rows] = came[part][...]
        if extra:
            outs[3][part, 0:rows] = held[part][...]
            outs[3][part, rows : 2 * rows] = came[part][...]


def join(held, came, extra):
    rows = held[0].shape[0]
    outs = [shape(2 * rows, THIRD)] * 3
    if extra:
        outs = outs + [jax.ShapeDtypeStruct((3, 2 * rows, THIRD), jnp.bfloat16)]
    return pl.pallas_call(
        functools.partial(join_kernel, extra),
        out_shape=outs,
        in_specs=whole(6),
        out_specs=whole(len(outs)),
        compiler_params=params(10),
        name="join_rows",
    )(*held, *came)


def gather_tokens(thirds, document_start, core_weight):
    came = [swap(thirds[p], ORDERS[p][0]) for p in range(3)]
    two = join(thirds, came, False)
    came = [swap(two[p], ORDERS[p][1]) for p in range(3)]
    *came, document_start = lax.optimization_barrier((*came, document_start))
    *four, packed = join(two, came, True)
    late = [swap(four[p], ORDERS[p][2]) for p in range(3)]
    other = swap(packed, CC)
    tables = make_tables(document_start)
    *late, cosine, sine, position, start, offset, where, core_weight = lax.optimization_barrier(
        (*late, *tables, core_weight)
    )
    both_weight = swap_y_both_ways(core_weight)
    other_late = [swap(late[p], CC) for p in range(3)]
    return (four, late, other, other_late), cosine, sine, where, position, start, offset, core_weight, both_weight


def rotate(raw, gain, cosine, sine):
    inverse = lax.rsqrt(jnp.mean(raw * raw, axis=-1, keepdims=True) + epsilon)
    scaled = raw * inverse * gain
    turned = pltpu.roll(scaled, HD // 2, 1)
    return (scaled * cosine + turned * sine).astype(jnp.bfloat16)


def project_kernel(weight_count, *refs):
    x_refs = refs[0:10]
    w_refs = refs[10 : 10 + weight_count]
    gain_ref, cos_ref, sin_ref, out_ref = refs[10 + weight_count :]
    four, late, other, other_late = x_refs[0:3], x_refs[3:6], x_refs[6], x_refs[7:10]
    total = None
    for part in range(3):
        order = gathered_order(part)
        rows = []
        for core in range(2):
            for place in range(8):
                k = order.index(place)
                at = (k % 4) * ROWS
                if core == 0:
                    rows.append((four if k < 4 else late)[part][at : at + ROWS])
                elif k < 4:
                    rows.append(other[part, at : at + ROWS])
                else:
                    rows.append(other_late[part][at : at + ROWS])
        weights = [w[part * THIRD : (part + 1) * THIRD] for w in w_refs]
        product = jnp.dot(
            jnp.concatenate(rows, axis=0),
            jnp.concatenate(weights, axis=1) if weight_count == 2 else weights[0],
            preferred_element_type=jnp.float32,
        )
        total = product if part == 0 else total + product
    gain = gain_ref[...]
    out_ref[:, 0:HD] = rotate(total[:, 0:HD], gain, cos_ref[...], sin_ref[...])
    if weight_count == 1:
        out_ref[:, HD : 2 * HD] = rotate(total[:, HD : 2 * HD], gain, cos_ref[...], sin_ref[...])
    else:
        out_ref[:, HD : 2 * HD] = total[:, HD : 2 * HD].astype(jnp.bfloat16)


def project(pieces, weights, gain, cosine, sine, name):
    four, late, other, other_late = pieces
    return pl.pallas_call(
        functools.partial(project_kernel, len(weights)),
        out_shape=shape(BLOCK, 2 * HD),
        in_specs=whole(13 + len(weights)),
        out_specs=whole(1)[0],
        compiler_params=params(14),
        cost_estimate=pl.CostEstimate(
            flops=2 * BLOCK * D * 2 * HD, bytes_accessed=9000000, transcendentals=0
        ),
        name=name,
    )(*four, *late, other, *other_late, *weights, gain.reshape(1, HD), cosine, sine)


NEG = -1e30
TILE = 256


def move(value, step):
    return lax.ppermute(value, "ctx", [(c, (c + step) % 8) for c in range(8)])


def attend_kernel(distances, joint, first, last, *refs):
    where_ref, q_ref, position_ref, start_ref, offset_ref = refs[0:5]
    refs = refs[5:]
    blocks, refs = refs[: len(joint)], refs[len(joint) :]
    if not first:
        old_state, refs = refs[0:3], refs[3:]
    if last:
        out_refs, state = refs[0:2], refs[2:5]
    else:
        state = refs[0:3]
    top, total, acc = state
    block = where_ref[0]
    live = where_ref[1]
    rows_here = q_ref.shape[0]
    factor = math.log2(math.e) / math.sqrt(query_scalar)

    def step(distance, keys_ref, values_ref, source):
        opening = source is None
        keys = keys_ref[...]
        values = values_ref[...]
        key_index = offset_ref[...] + (block - distance) * BLOCK
        for tile in range(rows_here // TILE):
            rows = slice(tile * TILE, (tile + 1) * TILE)
            position = position_ref[rows]
            start = start_ref[rows]
            for head in range(2):
                scores = lax.dot_general(
                    q_ref[rows, head * HD : (head + 1) * HD],
                    keys,
                    (((1,), (1,)), ((), ())),
                    preferred_element_type=jnp.float32,
                )
                pieces = []
                for k in range(BLOCK // HD):
                    index = key_index[:, k * HD : (k + 1) * HD]
                    allowed = index >= start
                    if distance == 0:
                        allowed = allowed & (index <= position)
                    pieces.append(
                        jnp.where(allowed, scores[:, k * HD : (k + 1) * HD] * factor, NEG)
                    )
                best = jnp.maximum(
                    jnp.maximum(pieces[0], pieces[1]), jnp.maximum(pieces[2], pieces[3])
                )
                best = jnp.max(best, axis=-1, keepdims=True)
                if opening:
                    new = jnp.broadcast_to(best, (TILE, HD))
                else:
                    old = source[0][head, rows]
                    new = jnp.maximum(old, best)
                exps = [jnp.exp2(piece - new) for piece in pieces]
                sums = (exps[0] + exps[1]) + (exps[2] + exps[3])
                weights = jnp.concatenate([e.astype(jnp.bfloat16) for e in exps], axis=1)
                product = jnp.dot(weights, values, preferred_element_type=jnp.float32)
                if not opening:
                    fade = jnp.exp2(old - new)
                    sums = source[1][head, rows] * fade + sums
                    product = source[2][head, rows] * fade + product
                total[head, rows] = sums
                acc[head, rows] = product
                top[head, rows] = new

    def keep():
        for new_ref, old_ref in zip(state, old_state):
            new_ref[...] = old_ref[...]

    source = None if first else old_state
    k = 0
    for distance, whole_block in zip(distances, joint):
        if whole_block == 2:
            continue
        if whole_block:
            keys_ref = blocks[k].at[:, pl.ds(0, HD)]
            values_ref = blocks[k].at[:, pl.ds(HD, HD)]
            k += 1
        else:
            keys_ref, values_ref = blocks[k], blocks[k + 1]
            k += 2
        if distance == 0:
            step(0, keys_ref, values_ref, None)
        else:
            pl.when(distance < live)(
                functools.partial(step, distance, keys_ref, values_ref, source)
            )
            if source is not state:
                pl.when(distance >= live)(keep)
        source = state
    if last:
        for head in range(2):
            for quarter in range(2):
                here = slice(quarter * 128, (quarter + 1) * 128)
                denominator = jnp.sum(total[head, here], axis=-1, keepdims=True)
                out_refs[quarter][:, head * HD : (head + 1) * HD] = (
                    acc[head, here] / denominator
                ).astype(jnp.bfloat16)


def attend(tables, query, distances, joint, blocks, state, last, half=None):
    where, position, start, offset = tables
    first = state is None
    state = () if first else tuple(state)
    rows_here = BLOCK // 2 if last else BLOCK
    state_shape = jax.ShapeDtypeStruct((2, rows_here, HD), jnp.float32)
    if last:
        out_shape, out_specs = [shape(128, 2 * HD)] * 2, whole(2)
        scratch = [pltpu.VMEM((2, rows_here, HD), jnp.float32)] * 3
        row_specs = [
            pl.BlockSpec((rows_here, 2 * HD), lambda k: (half, 0)),
            pl.BlockSpec((rows_here, HD), lambda k: (half, 0)),
            pl.BlockSpec((rows_here, HD), lambda k: (half, 0)),
        ]
        state_specs = [pl.BlockSpec((2, rows_here, HD), lambda k: (0, half, 0))] * 3
    else:
        out_shape, out_specs = [state_shape] * 3, whole(3)
        scratch = []
        row_specs = whole(3)
        state_specs = whole(3)
    return pl.pallas_call(
        functools.partial(attend_kernel, distances, joint, first, last),
        out_shape=out_shape,
        grid=(1,) if last else (),
        in_specs=[pl.BlockSpec(memory_space=pltpu.SMEM)]
        + row_specs
        + whole(1 + len(blocks))
        + (state_specs if state else []),
        out_specs=out_specs,
        scratch_shapes=scratch,
        compiler_params=params(10),
        cost_estimate=pl.CostEstimate(
            flops=800000000 * len(distances), bytes_accessed=3000000, transcendentals=1000000
        ),
        name="attend",
    )(where, query, position, start, offset, *blocks, *state)


def halves_kernel(keys_ref, values_ref, key_out, value_out):
    key_out[...] = keys_ref[:, 0:HD]
    value_out[...] = values_ref[:, HD : 2 * HD]


def take_halves(keys, values):
    return pl.pallas_call(
        halves_kernel,
        out_shape=[shape(BLOCK, HD)] * 2,
        in_specs=whole(2),
        out_specs=whole(2),
        compiler_params=params(4),
        name="take_halves",
    )(keys, values)


def share_and_attend(rows, make_query, tables, output_weight, core_weight, both_weight):
    tie = lax.optimization_barrier

    def onward(forward, backward):
        return move(forward, 1), move(backward, -1)

    one, back_one = onward(rows, rows)
    query = make_query()
    state = attend(tables, query, (0,), (1,), [rows], None, False)
    one, back_one, state = tie((one, back_one, state))
    two, back_two = onward(one, back_one)
    state = attend(tables, query, (1,), (1,), [one], state, False)
    two, back_two, state = tie((two, back_two, state))
    three, back_three = onward(two, back_two)
    state = attend(tables, query, (2, 6), (1, 1), [two, back_two], state, False)
    three, back_three, state, both_weight = tie((three, back_three, state, both_weight))
    y_weight = swap(both_weight, CC)
    key_half, value_half = take_halves(three, back_three)
    key_far = move(key_half, 1)
    value_far = move(value_half, -1)
    state = attend(tables, query, (3, 5), (1, 1), [three, back_three], state, False)
    key_far, value_far, state = tie((key_far, value_far, state))
    to_core, to_both = attend(tables, query, (4,), (0, 2), [key_far, value_far], state, True, 1)
    mine, to_y = attend(tables, query, (4,), (0, 2), [key_far, value_far], state, True, 0)
    parts = [mine, swap(to_core, CC), swap(to_y, YY), swap(to_both, CC ^ YY)]
    return parts, [output_weight, core_weight, y_weight, both_weight]


HALF = D // 2
CHUNK = 384
X_ORDERS = ((XA, XB), (XB, XA))


def output_kernel(part, *refs):
    rows, weights, keeps, goes = refs[0:4], refs[4:8], refs[8], refs[9]
    for chunk in range(HALF // CHUNK):
        here = slice(part * HALF + chunk * CHUNK, part * HALF + (chunk + 1) * CHUNK)
        summed = jnp.zeros((128, CHUNK), jnp.float32)
        for row, weight in zip(rows, weights):
            group = jnp.dot(row[...], weight[:, here], preferred_element_type=jnp.float32)
            summed = summed + group.astype(jnp.bfloat16).astype(jnp.float32)
        summed = summed.astype(jnp.bfloat16)
        to = slice(chunk * CHUNK, (chunk + 1) * CHUNK)
        bit = BITS[X_ORDERS[part][0]]
        for place in range(4):
            out = goes if place & bit else keeps
            at = (place >> 1 if bit == 1 else place & 1) * ROWS
            out[at : at + ROWS, to] = summed[place * ROWS : (place + 1) * ROWS]


def project_out(part, rows, weights):
    return pl.pallas_call(
        functools.partial(output_kernel, part),
        out_shape=[shape(64, HALF)] * 2,
        in_specs=whole(8),
        out_specs=whole(2),
        compiler_params=params(16),
        cost_estimate=pl.CostEstimate(
            flops=2 * 128 * 1024 * HALF, bytes_accessed=6500000, transcendentals=0
        ),
        name="project_out",
    )(*rows, *weights)


def fold_kernel(*refs):
    kept, came, outs = refs[0:2], refs[2:4], refs[4:]
    for part in range(2):
        summed = (
            kept[part][...].astype(jnp.float32) + came[part][...].astype(jnp.float32)
        ).astype(jnp.bfloat16)
        outs[2 * part][...] = summed[0:ROWS]
        outs[2 * part + 1][...] = summed[ROWS : 2 * ROWS]


def fold(kept, came):
    return pl.pallas_call(
        fold_kernel,
        out_shape=[shape(ROWS, HALF)] * 4,
        in_specs=whole(4),
        out_specs=whole(4),
        compiler_params=params(8),
        name="fold_rows",
    )(*kept, *came)


def finish_kernel(residual_ref, gain_ref, *refs):
    kept, came, out, sums = refs[0:2], refs[2:4], refs[4], refs[5]
    square = jnp.zeros((ROWS, HD), jnp.float32)
    for part in range(2):
        for k in range(HALF // HD):
            here = slice(k * HD, (k + 1) * HD)
            summed = kept[part][:, here].astype(jnp.float32) + came[part][:, here].astype(
                jnp.float32
            )
            at = part * HALF + k * HD
            sums[:, at : at + HD] = summed
            square = square + summed * summed
    inverse = lax.rsqrt(jnp.sum(square, axis=-1, keepdims=True) / D + epsilon)
    for k in range(D // HD):
        here = slice(k * HD, (k + 1) * HD)
        out[:, here] = (
            residual_ref[:, here].astype(jnp.float32)
            + sums[:, here] * inverse * gain_ref[k : k + 1]
        ).astype(jnp.bfloat16)


def finish(residual, gain, kept, came):
    return pl.pallas_call(
        finish_kernel,
        out_shape=shape(ROWS, D),
        in_specs=whole(6),
        out_specs=whole(1)[0],
        scratch_shapes=[pltpu.VMEM((ROWS, D), jnp.float32)],
        compiler_params=params(6),
        name="finish",
    )(residual, gain.reshape(D // HD, HD), *kept, *came)


def reduce_tokens(rows, weights):
    kept, came = [], []
    for part in range(2):
        keeps, goes = project_out(part, rows, weights)
        kept.append(keeps)
        came.append(swap(goes, X_ORDERS[part][0]))
    halves = fold(kept, came)
    came = [swap(halves[2 * part + 1], X_ORDERS[part][1]) for part in range(2)]
    return halves[0::2], came


def body(
    residual_in,
    document_start,
    input_gain,
    query_weight,
    key_weight,
    value_weight,
    query_gain,
    key_gain,
    output_weight,
    post_gain,
):
    thirds = norm_rows(residual_in, input_gain)

    pieces, cosine, sine, where, position_wide, start_wide, offset, core_weight, both_weight = gather_tokens(
        thirds,
        document_start,
        swap(output_weight, CC),
    )
    tables = (where, position_wide, start_wide, offset)
    rows = project(pieces, [key_weight, value_weight], key_gain, cosine, sine, "project_kv")
    parts, weights = share_and_attend(
        rows,
        lambda: project(pieces, [query_weight], query_gain, cosine, sine, "project_q"),
        tables,
        output_weight,
        core_weight,
        both_weight,
    )
    kept, came = reduce_tokens(parts, weights)
    return finish(residual_in, post_gain, kept, came)


def solution(mesh):
    return jax.shard_map(
        body,
        mesh=mesh,
        in_specs=(
            P(("docs", "ctx", "mp"), None),
            P(("docs", "ctx")),
            P(),
            P(None, "mp"),
            P(None, "mp"),
            P(None, "mp"),
            P(),
            P(),
            P("mp", None),
            P(),
        ),
        out_specs=P(("docs", "ctx", "mp"), None),
        check_vma=False,
    )
```

```python
import functools
import math

import jax
import jax.numpy as jnp
import numpy as np
from jax import lax
from jax.experimental import pallas as pl
from jax.experimental.pallas import tpu as pltpu
from jax.sharding import PartitionSpec as P

query_scalar = 168.0
rope_base = 1000000.0
rope_factor = 8.0
epsilon = 1e-06

D = 5376
THIRD = D // 3
HD = 128
ROWS = 32
BLOCK = 512

XA, XB, YY, CC = 2, 6, 8, 1
ORDERS = ((XA, XB, YY), (XB, YY, XA), (YY, XA, XB))
BITS = {XA: 1, XB: 2, YY: 4}


def mp_mask(index):
    return (XA if index & 1 else 0) ^ (XB if index & 2 else 0) ^ (YY if index & 4 else 0)


def gathered_order(part):
    first, second, third = (BITS[link] for link in ORDERS[part])
    return [
        (first if k & 1 else 0) | (second if k & 2 else 0) | (third if k & 4 else 0)
        for k in range(8)
    ]


def swap(value, link):
    return lax.ppermute(value, "mp", [(m, m ^ link) for m in range(16)])


def swap_y_both_ways(value):
    return lax.ppermute(
        value,
        ("docs", "mp"),
        [(d * 16 + m, (d ^ (m & 1)) * 16 + (m ^ YY)) for d in range(2) for m in range(16)],
    )


def whole(count):
    return [pl.BlockSpec(memory_space=pltpu.VMEM)] * count


def params(mebibytes):
    return pltpu.CompilerParams(vmem_limit_bytes=mebibytes * 1024 * 1024)


def shape(rows, columns, dtype=jnp.bfloat16):
    return jax.ShapeDtypeStruct((rows, columns), dtype)


def norm_kernel(x_hbm, gain_hbm, *refs):
    outs, x_ref, gain_ref, sem = refs[0:3], refs[3], refs[4], refs[5]
    copies = [
        pltpu.make_async_copy(x_hbm, x_ref, sem.at[0]),
        pltpu.make_async_copy(gain_hbm, gain_ref, sem.at[1]),
    ]
    for copy in copies:
        copy.start()
    for copy in copies:
        copy.wait()
    square = jnp.zeros((ROWS, HD), jnp.float32)
    for k in range(D // HD):
        x = x_ref[:, k * HD : (k + 1) * HD].astype(jnp.float32)
        square = square + x * x
    inverse = lax.rsqrt(jnp.sum(square, axis=-1, keepdims=True) / D + epsilon)
    for part, out in enumerate(outs):
        for k in range(THIRD // HD):
            at = part * (THIRD // HD) + k
            x = x_ref[:, at * HD : (at + 1) * HD].astype(jnp.float32)
            out[:, k * HD : (k + 1) * HD] = (x * inverse * gain_ref[at : at + 1]).astype(
                jnp.bfloat16
            )


def norm_rows(residual, gain):
    return pl.pallas_call(
        norm_kernel,
        out_shape=[shape(ROWS, THIRD)] * 3,
        in_specs=[pl.BlockSpec(memory_space=pltpu.HBM)] * 2,
        out_specs=whole(3),
        scratch_shapes=[
            pltpu.VMEM((ROWS, D), jnp.bfloat16),
            pltpu.VMEM((D // HD, HD), jnp.float32),
            pltpu.SemaphoreType.DMA((2,)),
        ],
        compiler_params=params(4),
        name="norm_rows",
    )(residual, gain.reshape(D // HD, HD))


def tables_kernel(
    starts_ref,
    first_ref,
    frequency_ref,
    query_gain_ref,
    key_gain_ref,
    key_weight_ref,
    value_weight_ref,
    cos_ref,
    sin_ref,
    position_ref,
    start_ref,
    offset_ref,
    query_gain_out,
    key_gain_out,
    weight_out,
    where_ref,
    natural,
    sem,
):
    copies = [
        pltpu.make_async_copy(source, weight_out.at[:, pl.ds(k * HD, HD)], sem.at[k])
        for k, source in enumerate((key_weight_ref, value_weight_ref))
    ]
    for copy in copies:
        copy.start()
    query_gain_out[...] = query_gain_ref[...]
    key_gain_out[...] = key_gain_ref[...]
    mine = lax.axis_index("mp")
    block = lax.axis_index("ctx")
    row = lax.broadcasted_iota(jnp.int32, (HD, HD), 0)
    lane = lax.broadcasted_iota(jnp.int32, (HD, HD), 1)
    for k in range(BLOCK // HD):
        spread = jnp.broadcast_to(starts_ref[k : k + 1].astype(jnp.float32), (HD, HD))
        column = jnp.sum(jnp.where(row == lane, spread, 0.0), axis=-1, keepdims=True)
        natural[k * HD : (k + 1) * HD] = jnp.broadcast_to(column, (HD, HD)).astype(jnp.int32)
    inner = lax.broadcasted_iota(jnp.int32, (ROWS, HD), 0)
    along = lax.broadcasted_iota(jnp.int32, (1, BLOCK), 1)
    offset = along
    sign = jnp.where(
        lax.broadcasted_iota(jnp.int32, (ROWS, HD), 1) < HD // 2, -1.0, 1.0
    )
    for k in range(16):
        owner = mine ^ (mp_mask(k & 7) ^ (k >> 3))
        here = slice(k * ROWS, (k + 1) * ROWS)
        start = natural[pl.ds(pl.multiple_of(owner * ROWS, ROWS), ROWS)]
        position = inner + (block * BLOCK + owner * ROWS)
        start_ref[here] = start
        position_ref[here] = position
        angles = ((position - start).astype(jnp.float32) / rope_factor) * frequency_ref[...]
        cos_ref[here] = jnp.cos(angles)
        sin_ref[here] = jnp.sin(angles) * sign
        inside = (along >= k * ROWS) & (along < (k + 1) * ROWS)
        offset = jnp.where(inside, along + (owner - k) * ROWS, offset)
    offset_ref[...] = offset
    where_ref[0] = block
    where_ref[1] = block - (first_ref[0] >> 9) + 1
    for copy in copies:
        copy.wait()


def make_tables(document_start, query_gain, key_gain, key_weight, value_weight):
    frequency = np.float32(rope_base) ** (
        -(np.arange(HD // 2, dtype=np.float32) * np.float32(2.0) / np.float32(HD))
    )
    frequency = jnp.asarray(np.concatenate([frequency, frequency])[None, :], jnp.float32)
    wide = lambda kind: jax.ShapeDtypeStruct((BLOCK, HD), kind)
    return pl.pallas_call(
        tables_kernel,
        out_shape=[
            wide(jnp.float32),
            wide(jnp.float32),
            wide(jnp.int32),
            wide(jnp.int32),
            jax.ShapeDtypeStruct((1, BLOCK), jnp.int32),
            shape(1, HD, jnp.float32),
            shape(1, HD, jnp.float32),
            shape(D, 2 * HD),
            jax.ShapeDtypeStruct((2,), jnp.int32),
        ],
        in_specs=[
            pl.BlockSpec(memory_space=pltpu.VMEM),
            pl.BlockSpec(memory_space=pltpu.SMEM),
            *whole(3),
            pl.BlockSpec(memory_space=pltpu.HBM),
            pl.BlockSpec(memory_space=pltpu.HBM),
        ],
        out_specs=whole(8) + [pl.BlockSpec(memory_space=pltpu.SMEM)],
        scratch_shapes=[pltpu.VMEM((BLOCK, HD), jnp.int32), pltpu.SemaphoreType.DMA((2,))],
        compiler_params=params(7),
        cost_estimate=pl.CostEstimate(
            flops=4000000, bytes_accessed=1000000, transcendentals=131072
        ),
        name="tables",
    )(
        document_start.reshape(BLOCK // HD, HD),
        document_start,
        frequency,
        query_gain.reshape(1, HD),
        key_gain.reshape(1, HD),
        key_weight,
        value_weight,
    )


def join_kernel(extra, *refs):
    held, came, outs = refs[0:3], refs[3:6], refs[6:]
    for part in range(3):
        rows = held[part].shape[0]
        outs[part][0:rows] = held[part][...]
        outs[part][rows : 2 * rows] = came[part][...]
        if extra:
            outs[3][part, 0:rows] = held[part][...]
            outs[3][part, rows : 2 * rows] = came[part][...]


def join(held, came, extra):
    rows = held[0].shape[0]
    outs = [shape(2 * rows, THIRD)] * 3
    if extra:
        outs = outs + [jax.ShapeDtypeStruct((3, 2 * rows, THIRD), jnp.bfloat16)]
    return pl.pallas_call(
        functools.partial(join_kernel, extra),
        out_shape=outs,
        in_specs=whole(6),
        out_specs=whole(len(outs)),
        compiler_params=params(10),
        name="join_rows",
    )(*held, *came)


def gather_tokens(thirds, document_start, core_weight, *small):
    came = [swap(thirds[p], ORDERS[p][0]) for p in range(3)]
    two = join(thirds, came, False)
    came = [swap(two[p], ORDERS[p][1]) for p in range(3)]
    *came, document_start, core_weight = lax.optimization_barrier(
        (*came, document_start, core_weight)
    )
    *four, packed = join(two, came, True)
    late = [swap(four[p], ORDERS[p][2]) for p in range(3)]
    other = swap(packed, CC)
    tables = make_tables(document_start, *small)
    other_late = [swap(late[p], CC) for p in range(3)]
    held = lax.optimization_barrier((*late, *tables, core_weight))
    late, tables, core_weight = held[0:3], held[3:12], held[12]
    both_weight = swap_y_both_ways(core_weight)
    return (four, late, other, other_late), tables, core_weight, both_weight


def rotate(raw, gain, cosine, sine):
    inverse = lax.rsqrt(jnp.mean(raw * raw, axis=-1, keepdims=True) + epsilon)
    scaled = raw * inverse * gain
    turned = pltpu.roll(scaled, HD // 2, 1)
    return (scaled * cosine + turned * sine).astype(jnp.bfloat16)


def project_kernel(both, *refs):
    x_refs = refs[0:10]
    w_ref, gain_ref, cos_ref, sin_ref, out_ref = refs[10:]
    four, late, other, other_late = x_refs[0:3], x_refs[3:6], x_refs[6], x_refs[7:10]
    total = None
    for part in range(3):
        order = gathered_order(part)
        rows = []
        for core in range(2):
            for place in range(8):
                k = order.index(place)
                at = (k % 4) * ROWS
                if core == 0:
                    rows.append((four if k < 4 else late)[part][at : at + ROWS])
                elif k < 4:
                    rows.append(other[part, at : at + ROWS])
                else:
                    rows.append(other_late[part][at : at + ROWS])
        product = jnp.dot(
            jnp.concatenate(rows, axis=0),
            w_ref[part * THIRD : (part + 1) * THIRD],
            preferred_element_type=jnp.float32,
        )
        total = product if part == 0 else total + product
    gain = gain_ref[...]
    out_ref[:, 0:HD] = rotate(total[:, 0:HD], gain, cos_ref[...], sin_ref[...])
    if both:
        out_ref[:, HD : 2 * HD] = rotate(total[:, HD : 2 * HD], gain, cos_ref[...], sin_ref[...])
    else:
        out_ref[:, HD : 2 * HD] = total[:, HD : 2 * HD].astype(jnp.bfloat16)


def project(pieces, weight, gain, cosine, sine, both, name):
    four, late, other, other_late = pieces
    return pl.pallas_call(
        functools.partial(project_kernel, both),
        out_shape=shape(BLOCK, 2 * HD),
        in_specs=whole(14),
        out_specs=whole(1)[0],
        compiler_params=params(14),
        cost_estimate=pl.CostEstimate(
            flops=2 * BLOCK * D * 2 * HD, bytes_accessed=9000000, transcendentals=0
        ),
        name=name,
    )(*four, *late, other, *other_late, weight, gain, cosine, sine)


NEG = -1e30
TILE = 256


def move(value, step):
    return lax.ppermute(value, "ctx", [(c, (c + step) % 8) for c in range(8)])


def attend_kernel(distances, joint, first, last, *refs):
    where_ref, q_ref, position_ref, start_ref, offset_ref = refs[0:5]
    refs = refs[5:]
    blocks, refs = refs[: len(joint)], refs[len(joint) :]
    if not first:
        old_state, refs = refs[0:3], refs[3:]
    if last:
        out_refs, state = refs[0:4], refs[4:7]
    else:
        state = refs[0:3]
    top, total, acc = state
    block = where_ref[0]
    live = where_ref[1]
    rows_here = q_ref.shape[0]
    factor = math.log2(math.e) / math.sqrt(query_scalar)

    def step(distance, keys_ref, values_ref, source):
        opening = source is None
        keys = keys_ref[...]
        values = values_ref[...]
        key_index = offset_ref[...] + (block - distance) * BLOCK
        for tile in range(rows_here // TILE):
            rows = slice(tile * TILE, (tile + 1) * TILE)
            position = position_ref[rows]
            start = start_ref[rows]
            for head in range(2):
                scores = lax.dot_general(
                    q_ref[rows, head * HD : (head + 1) * HD],
                    keys,
                    (((1,), (1,)), ((), ())),
                    preferred_element_type=jnp.float32,
                )
                pieces = []
                for k in range(BLOCK // HD):
                    index = key_index[:, k * HD : (k + 1) * HD]
                    allowed = index >= start
                    if distance == 0:
                        allowed = allowed & (index <= position)
                    pieces.append(
                        jnp.where(allowed, scores[:, k * HD : (k + 1) * HD] * factor, NEG)
                    )
                best = jnp.maximum(
                    jnp.maximum(pieces[0], pieces[1]), jnp.maximum(pieces[2], pieces[3])
                )
                best = jnp.max(best, axis=-1, keepdims=True)
                if opening:
                    new = jnp.broadcast_to(best, (TILE, HD))
                else:
                    old = source[0][head, rows]
                    new = jnp.maximum(old, best)
                exps = [jnp.exp2(piece - new) for piece in pieces]
                sums = (exps[0] + exps[1]) + (exps[2] + exps[3])
                weights = jnp.concatenate([e.astype(jnp.bfloat16) for e in exps], axis=1)
                product = jnp.dot(weights, values, preferred_element_type=jnp.float32)
                if not opening:
                    fade = jnp.exp2(old - new)
                    sums = source[1][head, rows] * fade + sums
                    product = source[2][head, rows] * fade + product
                total[head, rows] = sums
                acc[head, rows] = product
                top[head, rows] = new

    def keep():
        for new_ref, old_ref in zip(state, old_state):
            new_ref[...] = old_ref[...]

    source = None if first else old_state
    k = 0
    for distance, whole_block in zip(distances, joint):
        if whole_block:
            keys_ref = blocks[k].at[:, pl.ds(0, HD)]
            values_ref = blocks[k].at[:, pl.ds(HD, HD)]
            k += 1
        else:
            keys_ref, values_ref = blocks[k], blocks[k + 1]
            k += 2
        if distance == 0:
            step(0, keys_ref, values_ref, None)
        else:
            pl.when(distance < live)(
                functools.partial(step, distance, keys_ref, values_ref, source)
            )
            if source is not state:
                pl.when(distance >= live)(keep)
        source = state
    if last:
        for head in range(2):
            for quarter in range(4):
                here = slice(quarter * 128, (quarter + 1) * 128)
                denominator = jnp.sum(total[head, here], axis=-1, keepdims=True)
                out_refs[quarter][:, head * HD : (head + 1) * HD] = (
                    acc[head, here] / denominator
                ).astype(jnp.bfloat16)


def attend(tables, query, distances, joint, blocks, state, last):
    where, position, start, offset = tables
    first = state is None
    state = () if first else tuple(state)
    state_shape = jax.ShapeDtypeStruct((2, BLOCK, HD), jnp.float32)
    if last:
        out_shape, out_specs = [shape(128, 2 * HD)] * 4, whole(4)
        scratch = [pltpu.VMEM((2, BLOCK, HD), jnp.float32)] * 3
    else:
        out_shape, out_specs = [state_shape] * 3, whole(3)
        scratch = []
    return pl.pallas_call(
        functools.partial(attend_kernel, distances, joint, first, last),
        out_shape=out_shape,
        in_specs=[pl.BlockSpec(memory_space=pltpu.SMEM)]
        + whole(4 + len(blocks) + len(state)),
        out_specs=out_specs,
        scratch_shapes=scratch,
        compiler_params=params(10),
        cost_estimate=pl.CostEstimate(
            flops=800000000 * len(distances), bytes_accessed=3000000, transcendentals=1000000
        ),
        name="attend",
    )(where, query, position, start, offset, *blocks, *state)


def halves_kernel(keys_ref, values_ref, key_out, value_out):
    key_out[...] = keys_ref[:, 0:HD]
    value_out[...] = values_ref[:, HD : 2 * HD]


def take_halves(keys, values):
    return pl.pallas_call(
        halves_kernel,
        out_shape=[shape(BLOCK, HD)] * 2,
        in_specs=whole(2),
        out_specs=whole(2),
        compiler_params=params(4),
        name="take_halves",
    )(keys, values)


def share_and_attend(rows, make_query, tables, output_weight, core_weight, both_weight):
    tie = lax.optimization_barrier

    def onward(forward, backward):
        return move(forward, 1), move(backward, -1)

    one, back_one = onward(rows, rows)
    query = make_query()
    state = attend(tables, query, (0,), (1,), [rows], None, False)
    one, back_one, state = tie((one, back_one, state))
    two, back_two = onward(one, back_one)
    state = attend(tables, query, (1,), (1,), [one], state, False)
    two, back_two, state = tie((two, back_two, state))
    three, back_three = onward(two, back_two)
    state = attend(tables, query, (2, 6), (1, 1), [two, back_two], state, False)
    three, back_three, state, both_weight = tie((three, back_three, state, both_weight))
    y_weight = swap(both_weight, CC)
    key_half, value_half = take_halves(three, back_three)
    key_far = lax.ppermute(key_half, "ctx", [(3, 4), (4, 5), (5, 6)])
    value_far = lax.ppermute(value_half, "ctx", [(5, 4), (6, 5), (7, 6)])
    state = attend(tables, query, (3, 5), (1, 1), [three, back_three], state, False)
    key_far, value_far, state = tie((key_far, value_far, state))
    mine, to_y, to_core, to_both = attend(tables, query, (4,), (0, 2), [key_far, value_far], state, True)
    parts = [mine, swap(to_core, CC), swap(to_y, YY), swap(to_both, CC ^ YY)]
    return parts, [output_weight, core_weight, y_weight, both_weight]


HALF = D // 2
CHUNK = 384
X_ORDERS = ((XA, XB), (XB, XA))


def output_kernel(part, *refs):
    rows, weights, keeps, goes = refs[0:4], refs[4:8], refs[8], refs[9]
    for chunk in range(HALF // CHUNK):
        here = slice(part * HALF + chunk * CHUNK, part * HALF + (chunk + 1) * CHUNK)
        summed = jnp.zeros((128, CHUNK), jnp.float32)
        for row, weight in zip(rows, weights):
            group = jnp.dot(row[...], weight[:, here], preferred_element_type=jnp.float32)
            summed = summed + group.astype(jnp.bfloat16).astype(jnp.float32)
        summed = summed.astype(jnp.bfloat16)
        to = slice(chunk * CHUNK, (chunk + 1) * CHUNK)
        bit = BITS[X_ORDERS[part][0]]
        for place in range(4):
            out = goes if place & bit else keeps
            at = (place >> 1 if bit == 1 else place & 1) * ROWS
            out[at : at + ROWS, to] = summed[place * ROWS : (place + 1) * ROWS]


def project_out(part, rows, weights):
    return pl.pallas_call(
        functools.partial(output_kernel, part),
        out_shape=[shape(64, HALF)] * 2,
        in_specs=whole(8),
        out_specs=whole(2),
        compiler_params=params(16),
        cost_estimate=pl.CostEstimate(
            flops=2 * 128 * 1024 * HALF, bytes_accessed=6500000, transcendentals=0
        ),
        name="project_out",
    )(*rows, *weights)


def fold_kernel(*refs):
    kept, came, outs = refs[0:2], refs[2:4], refs[4:]
    for part in range(2):
        summed = (
            kept[part][...].astype(jnp.float32) + came[part][...].astype(jnp.float32)
        ).astype(jnp.bfloat16)
        outs[2 * part][...] = summed[0:ROWS]
        outs[2 * part + 1][...] = summed[ROWS : 2 * ROWS]


def fold(kept, came):
    return pl.pallas_call(
        fold_kernel,
        out_shape=[shape(ROWS, HALF)] * 4,
        in_specs=whole(4),
        out_specs=whole(4),
        compiler_params=params(8),
        name="fold_rows",
    )(*kept, *came)


def finish_kernel(residual_ref, gain_ref, *refs):
    kept, came, out, sums = refs[0:2], refs[2:4], refs[4], refs[5]
    square = jnp.zeros((ROWS, HD), jnp.float32)
    for part in range(2):
        for k in range(HALF // HD):
            here = slice(k * HD, (k + 1) * HD)
            summed = kept[part][:, here].astype(jnp.float32) + came[part][:, here].astype(
                jnp.float32
            )
            at = part * HALF + k * HD
            sums[:, at : at + HD] = summed
            square = square + summed * summed
    inverse = lax.rsqrt(jnp.sum(square, axis=-1, keepdims=True) / D + epsilon)
    for k in range(D // HD):
        here = slice(k * HD, (k + 1) * HD)
        out[:, here] = (
            residual_ref[:, here].astype(jnp.float32)
            + sums[:, here] * inverse * gain_ref[k : k + 1]
        ).astype(jnp.bfloat16)


def finish(residual, gain, kept, came):
    return pl.pallas_call(
        finish_kernel,
        out_shape=shape(ROWS, D),
        in_specs=whole(6),
        out_specs=whole(1)[0],
        scratch_shapes=[pltpu.VMEM((ROWS, D), jnp.float32)],
        compiler_params=params(6),
        name="finish",
    )(residual, gain.reshape(D // HD, HD), *kept, *came)


def reduce_tokens(rows, weights):
    kept, came = [], []
    for part in range(2):
        keeps, goes = project_out(part, rows, weights)
        kept.append(keeps)
        came.append(swap(goes, X_ORDERS[part][0]))
    halves = fold(kept, came)
    came = [swap(halves[2 * part + 1], X_ORDERS[part][1]) for part in range(2)]
    return halves[0::2], came


def body(
    residual_in,
    document_start,
    input_gain,
    query_weight,
    key_weight,
    value_weight,
    query_gain,
    key_gain,
    output_weight,
    post_gain,
):
    thirds = norm_rows(residual_in, input_gain)

    pieces, made, core_weight, both_weight = gather_tokens(
        thirds,
        document_start,
        swap(output_weight, CC),
        query_gain,
        key_gain,
        key_weight,
        value_weight,
    )
    cosine, sine, position, start, offset, query_gain, key_gain, pair_weight, where = made
    rows = project(pieces, pair_weight, key_gain, cosine, sine, False, "project_kv")
    parts, weights = share_and_attend(
        rows,
        lambda: project(pieces, query_weight, query_gain, cosine, sine, True, "project_q"),
        (where, position, start, offset),
        output_weight,
        core_weight,
        both_weight,
    )
    kept, came = reduce_tokens(parts, weights)
    return finish(residual_in, post_gain, kept, came)


def solution(mesh):
    return jax.shard_map(
        body,
        mesh=mesh,
        in_specs=(
            P(("docs", "ctx", "mp"), None),
            P(("docs", "ctx")),
            P(),
            P(None, "mp"),
            P(None, "mp"),
            P(None, "mp"),
            P(),
            P(),
            P("mp", None),
            P(),
        ),
        out_specs=P(("docs", "ctx", "mp"), None),
        check_vma=False,
    )
```

```python
import functools
import math

import jax
import jax.numpy as jnp
import numpy as np
from jax import lax
from jax.experimental import pallas as pl
from jax.experimental.pallas import tpu as pltpu
from jax.sharding import PartitionSpec as P

query_scalar = 168.0
rope_base = 1000000.0
rope_factor = 8.0
epsilon = 1e-06

D = 5376
THIRD = D // 3
HD = 128
ROWS = 32
BLOCK = 512

XA, XB, YY, CC = 2, 6, 8, 1
ORDERS = ((XA, XB, YY), (XB, YY, XA), (YY, XA, XB))
BITS = {XA: 1, XB: 2, YY: 4}


def mp_mask(index):
    return (XA if index & 1 else 0) ^ (XB if index & 2 else 0) ^ (YY if index & 4 else 0)


def gathered_order(part):
    first, second, third = (BITS[link] for link in ORDERS[part])
    return [
        (first if k & 1 else 0) | (second if k & 2 else 0) | (third if k & 4 else 0)
        for k in range(8)
    ]


def swap(value, link):
    return lax.ppermute(value, "mp", [(m, m ^ link) for m in range(16)])


def swap_y_both_ways(value):
    return lax.ppermute(
        value,
        ("docs", "mp"),
        [(d * 16 + m, (d ^ (m & 1)) * 16 + (m ^ YY)) for d in range(2) for m in range(16)],
    )


def whole(count):
    return [pl.BlockSpec(memory_space=pltpu.VMEM)] * count


def params(mebibytes):
    return pltpu.CompilerParams(vmem_limit_bytes=mebibytes * 1024 * 1024)


def shape(rows, columns, dtype=jnp.bfloat16):
    return jax.ShapeDtypeStruct((rows, columns), dtype)


def norm_kernel(x_hbm, gain_hbm, *refs):
    outs, x_ref, gain_ref, sem = refs[0:3], refs[3], refs[4], refs[5]
    copies = [
        pltpu.make_async_copy(x_hbm, x_ref, sem.at[0]),
        pltpu.make_async_copy(gain_hbm, gain_ref, sem.at[1]),
    ]
    for copy in copies:
        copy.start()
    for copy in copies:
        copy.wait()
    square = jnp.zeros((ROWS, HD), jnp.float32)
    for k in range(D // HD):
        x = x_ref[:, k * HD : (k + 1) * HD].astype(jnp.float32)
        square = square + x * x
    inverse = lax.rsqrt(jnp.sum(square, axis=-1, keepdims=True) / D + epsilon)
    for part, out in enumerate(outs):
        for k in range(THIRD // HD):
            at = part * (THIRD // HD) + k
            x = x_ref[:, at * HD : (at + 1) * HD].astype(jnp.float32)
            out[:, k * HD : (k + 1) * HD] = (x * inverse * gain_ref[at : at + 1]).astype(
                jnp.bfloat16
            )


def norm_rows(residual, gain):
    return pl.pallas_call(
        norm_kernel,
        out_shape=[shape(ROWS, THIRD)] * 3,
        in_specs=[pl.BlockSpec(memory_space=pltpu.HBM)] * 2,
        out_specs=whole(3),
        scratch_shapes=[
            pltpu.VMEM((ROWS, D), jnp.bfloat16),
            pltpu.VMEM((D // HD, HD), jnp.float32),
            pltpu.SemaphoreType.DMA((2,)),
        ],
        compiler_params=params(4),
        name="norm_rows",
    )(residual, gain.reshape(D // HD, HD))


def tables_kernel(
    starts_ref,
    first_ref,
    frequency_ref,
    query_gain_ref,
    key_gain_ref,
    key_weight_ref,
    value_weight_ref,
    cos_ref,
    sin_ref,
    position_ref,
    start_ref,
    offset_ref,
    query_gain_out,
    key_gain_out,
    weight_out,
    where_ref,
    natural,
    sem,
):
    copies = [
        pltpu.make_async_copy(source, weight_out.at[:, pl.ds(k * HD, HD)], sem.at[k])
        for k, source in enumerate((key_weight_ref, value_weight_ref))
    ]
    for copy in copies:
        copy.start()
    query_gain_out[...] = query_gain_ref[...]
    key_gain_out[...] = key_gain_ref[...]
    mine = lax.axis_index("mp")
    block = lax.axis_index("ctx")
    row = lax.broadcasted_iota(jnp.int32, (HD, HD), 0)
    lane = lax.broadcasted_iota(jnp.int32, (HD, HD), 1)
    for k in range(BLOCK // HD):
        spread = jnp.broadcast_to(starts_ref[k : k + 1].astype(jnp.float32), (HD, HD))
        column = jnp.sum(jnp.where(row == lane, spread, 0.0), axis=-1, keepdims=True)
        natural[k * HD : (k + 1) * HD] = jnp.broadcast_to(column, (HD, HD)).astype(jnp.int32)
    inner = lax.broadcasted_iota(jnp.int32, (ROWS, HD), 0)
    along = lax.broadcasted_iota(jnp.int32, (1, BLOCK), 1)
    offset = along
    sign = jnp.where(
        lax.broadcasted_iota(jnp.int32, (ROWS, HD), 1) < HD // 2, -1.0, 1.0
    )
    for k in range(16):
        owner = mine ^ (mp_mask(k & 7) ^ (k >> 3))
        here = slice(k * ROWS, (k + 1) * ROWS)
        start = natural[pl.ds(pl.multiple_of(owner * ROWS, ROWS), ROWS)]
        position = inner + (block * BLOCK + owner * ROWS)
        start_ref[here] = start
        position_ref[here] = position
        angles = ((position - start).astype(jnp.float32) / rope_factor) * frequency_ref[...]
        cos_ref[here] = jnp.cos(angles)
        sin_ref[here] = jnp.sin(angles) * sign
        inside = (along >= k * ROWS) & (along < (k + 1) * ROWS)
        offset = jnp.where(inside, along + (owner - k) * ROWS, offset)
    offset_ref[...] = offset
    where_ref[0] = block
    where_ref[1] = block - (first_ref[0] >> 9) + 1
    for copy in copies:
        copy.wait()


def make_tables(document_start, query_gain, key_gain, key_weight, value_weight):
    frequency = np.float32(rope_base) ** (
        -(np.arange(HD // 2, dtype=np.float32) * np.float32(2.0) / np.float32(HD))
    )
    frequency = jnp.asarray(np.concatenate([frequency, frequency])[None, :], jnp.float32)
    wide = lambda kind: jax.ShapeDtypeStruct((BLOCK, HD), kind)
    return pl.pallas_call(
        tables_kernel,
        out_shape=[
            wide(jnp.float32),
            wide(jnp.float32),
            wide(jnp.int32),
            wide(jnp.int32),
            jax.ShapeDtypeStruct((1, BLOCK), jnp.int32),
            shape(1, HD, jnp.float32),
            shape(1, HD, jnp.float32),
            shape(D, 2 * HD),
            jax.ShapeDtypeStruct((2,), jnp.int32),
        ],
        in_specs=[
            pl.BlockSpec(memory_space=pltpu.VMEM),
            pl.BlockSpec(memory_space=pltpu.SMEM),
            *whole(3),
            pl.BlockSpec(memory_space=pltpu.HBM),
            pl.BlockSpec(memory_space=pltpu.HBM),
        ],
        out_specs=whole(8) + [pl.BlockSpec(memory_space=pltpu.SMEM)],
        scratch_shapes=[pltpu.VMEM((BLOCK, HD), jnp.int32), pltpu.SemaphoreType.DMA((2,))],
        compiler_params=params(7),
        cost_estimate=pl.CostEstimate(
            flops=4000000, bytes_accessed=1000000, transcendentals=131072
        ),
        name="tables",
    )(
        document_start.reshape(BLOCK // HD, HD),
        document_start,
        frequency,
        query_gain.reshape(1, HD),
        key_gain.reshape(1, HD),
        key_weight,
        value_weight,
    )


def join_kernel(extra, *refs):
    held, came, outs = refs[0:3], refs[3:6], refs[6:]
    for part in range(3):
        rows = held[part].shape[0]
        outs[part][0:rows] = held[part][...]
        outs[part][rows : 2 * rows] = came[part][...]
        if extra:
            outs[3][part, 0:rows] = held[part][...]
            outs[3][part, rows : 2 * rows] = came[part][...]


def join(held, came, extra):
    rows = held[0].shape[0]
    outs = [shape(2 * rows, THIRD)] * 3
    if extra:
        outs = outs + [jax.ShapeDtypeStruct((3, 2 * rows, THIRD), jnp.bfloat16)]
    return pl.pallas_call(
        functools.partial(join_kernel, extra),
        out_shape=outs,
        in_specs=whole(6),
        out_specs=whole(len(outs)),
        compiler_params=params(10),
        name="join_rows",
    )(*held, *came)


def gather_tokens(thirds, document_start, core_weight, *small):
    came = [swap(thirds[p], ORDERS[p][0]) for p in range(3)]
    two = join(thirds, came, False)
    came = [swap(two[p], ORDERS[p][1]) for p in range(3)]
    *came, document_start, core_weight = lax.optimization_barrier(
        (*came, document_start, core_weight)
    )
    *four, packed = join(two, came, True)
    late = [swap(four[p], ORDERS[p][2]) for p in range(3)]
    other = swap(packed, CC)
    tables = make_tables(document_start, *small)
    other_late = [swap(late[p], CC) for p in range(3)]
    held = lax.optimization_barrier((*late, *tables, core_weight, other))
    late, tables, core_weight, other = held[0:3], held[3:12], held[12], held[13]
    both_weight = swap_y_both_ways(core_weight)
    return (four, late, other, other_late), tables, core_weight, both_weight


def rotate(raw, gain, cosine, sine):
    inverse = lax.rsqrt(jnp.mean(raw * raw, axis=-1, keepdims=True) + epsilon)
    scaled = raw * inverse * gain
    turned = pltpu.roll(scaled, HD // 2, 1)
    return (scaled * cosine + turned * sine).astype(jnp.bfloat16)


def projected(x_refs, w_ref, cores):
    four, late = x_refs[0:3], x_refs[3:6]
    if 1 in cores:
        other, other_late = x_refs[6], x_refs[7:10]
    total = None
    for part in range(3):
        order = gathered_order(part)
        rows = []
        for core in cores:
            for place in range(8):
                k = order.index(place)
                at = (k % 4) * ROWS
                if core == 0:
                    rows.append((four if k < 4 else late)[part][at : at + ROWS])
                elif k < 4:
                    rows.append(other[part, at : at + ROWS])
                else:
                    rows.append(other_late[part][at : at + ROWS])
        product = jnp.dot(
            jnp.concatenate(rows, axis=0),
            w_ref[part * THIRD : (part + 1) * THIRD],
            preferred_element_type=jnp.float32,
        )
        total = product if part == 0 else total + product
    return total


def query_kernel(*refs):
    w_ref, gain_ref, cos_ref, sin_ref, out_ref = refs[10:]
    total = projected(refs[0:10], w_ref, (0, 1))
    gain = gain_ref[...]
    for head in range(2):
        here = slice(head * HD, (head + 1) * HD)
        out_ref[:, here] = rotate(total[:, here], gain, cos_ref[...], sin_ref[...])


def key_value_kernel(core, *refs):
    count = 10 if core else 6
    w_ref, gain_ref, cos_ref, sin_ref = refs[count : count + 4]
    out_ref = refs[-1]
    total = projected(refs[0:count], w_ref, (core,))
    table = slice(core * 256, (core + 1) * 256)
    here = table if core else slice(0, 256)
    if core:
        out_ref[0:256] = refs[count + 4][...]
    out_ref[here, 0:HD] = rotate(
        total[:, 0:HD], gain_ref[...], cos_ref[table], sin_ref[table]
    )
    out_ref[here, HD : 2 * HD] = total[:, HD : 2 * HD].astype(jnp.bfloat16)


def project_call(kernel, rows, flops, name, *operands):
    return pl.pallas_call(
        kernel,
        out_shape=shape(rows, 2 * HD),
        in_specs=whole(len(operands)),
        out_specs=whole(1)[0],
        compiler_params=params(14),
        cost_estimate=pl.CostEstimate(flops=flops, bytes_accessed=9000000, transcendentals=0),
        name=name,
    )(*operands)


def project_query(pieces, weight, gain, cosine, sine):
    four, late, other, other_late = pieces
    flops = 2 * BLOCK * D * 2 * HD
    return project_call(
        query_kernel, BLOCK, flops, "project_q",
        *four, *late, other, *other_late, weight, gain, cosine, sine,
    )


def project_key_value(pieces, weight, gain, cosine, sine):
    four, late, other, other_late = pieces
    flops = BLOCK * D * 2 * HD
    mine = project_call(
        functools.partial(key_value_kernel, 0), 256, flops, "project_kv_mine",
        *four, *late, weight, gain, cosine, sine,
    )
    return project_call(
        functools.partial(key_value_kernel, 1), BLOCK, flops, "project_kv",
        *four, *late, other, *other_late, weight, gain, cosine, sine, mine,
    )


NEG = -1e30
TILE = 256


def move(value, step):
    return lax.ppermute(value, "ctx", [(c, (c + step) % 8) for c in range(8)])


def attend_kernel(distances, joint, first, last, *refs):
    where_ref, q_ref, position_ref, start_ref, offset_ref = refs[0:5]
    refs = refs[5:]
    blocks, refs = refs[: len(joint)], refs[len(joint) :]
    if not first:
        old_state, refs = refs[0:3], refs[3:]
    if last:
        out_refs, state = refs[0:4], refs[4:7]
    else:
        state = refs[0:3]
    top, total, acc = state
    block = where_ref[0]
    live = where_ref[1]
    rows_here = q_ref.shape[0]
    factor = math.log2(math.e) / math.sqrt(query_scalar)

    def step(distance, keys_ref, values_ref, source):
        opening = source is None
        keys = keys_ref[...]
        values = values_ref[...]
        key_index = offset_ref[...] + (block - distance) * BLOCK
        for tile in range(rows_here // TILE):
            rows = slice(tile * TILE, (tile + 1) * TILE)
            position = position_ref[rows]
            start = start_ref[rows]
            for head in range(2):
                scores = lax.dot_general(
                    q_ref[rows, head * HD : (head + 1) * HD],
                    keys,
                    (((1,), (1,)), ((), ())),
                    preferred_element_type=jnp.float32,
                )
                pieces = []
                for k in range(BLOCK // HD):
                    index = key_index[:, k * HD : (k + 1) * HD]
                    allowed = index >= start
                    if distance == 0:
                        allowed = allowed & (index <= position)
                    pieces.append(
                        jnp.where(allowed, scores[:, k * HD : (k + 1) * HD] * factor, NEG)
                    )
                best = jnp.maximum(
                    jnp.maximum(pieces[0], pieces[1]), jnp.maximum(pieces[2], pieces[3])
                )
                best = jnp.max(best, axis=-1, keepdims=True)
                if opening:
                    new = jnp.broadcast_to(best, (TILE, HD))
                else:
                    old = source[0][head, rows]
                    new = jnp.maximum(old, best)
                exps = [jnp.exp2(piece - new) for piece in pieces]
                sums = (exps[0] + exps[1]) + (exps[2] + exps[3])
                weights = jnp.concatenate([e.astype(jnp.bfloat16) for e in exps], axis=1)
                product = jnp.dot(weights, values, preferred_element_type=jnp.float32)
                if not opening:
                    fade = jnp.exp2(old - new)
                    sums = source[1][head, rows] * fade + sums
                    product = source[2][head, rows] * fade + product
                total[head, rows] = sums
                acc[head, rows] = product
                top[head, rows] = new

    def keep():
        for new_ref, old_ref in zip(state, old_state):
            new_ref[...] = old_ref[...]

    source = None if first else old_state
    k = 0
    for distance, whole_block in zip(distances, joint):
        if whole_block:
            keys_ref = blocks[k].at[:, pl.ds(0, HD)]
            values_ref = blocks[k].at[:, pl.ds(HD, HD)]
            k += 1
        else:
            keys_ref, values_ref = blocks[k], blocks[k + 1]
            k += 2
        if distance == 0:
            step(0, keys_ref, values_ref, None)
        else:
            pl.when(distance < live)(
                functools.partial(step, distance, keys_ref, values_ref, source)
            )
            if source is not state:
                pl.when(distance >= live)(keep)
        source = state
    if last:
        for head in range(2):
            for quarter in range(4):
                here = slice(quarter * 128, (quarter + 1) * 128)
                denominator = jnp.sum(total[head, here], axis=-1, keepdims=True)
                out_refs[quarter][:, head * HD : (head + 1) * HD] = (
                    acc[head, here] / denominator
                ).astype(jnp.bfloat16)


def attend(tables, query, distances, joint, blocks, state, last):
    where, position, start, offset = tables
    first = state is None
    state = () if first else tuple(state)
    state_shape = jax.ShapeDtypeStruct((2, BLOCK, HD), jnp.float32)
    if last:
        out_shape, out_specs = [shape(128, 2 * HD)] * 4, whole(4)
        scratch = [pltpu.VMEM((2, BLOCK, HD), jnp.float32)] * 3
    else:
        out_shape, out_specs = [state_shape] * 3, whole(3)
        scratch = []
    return pl.pallas_call(
        functools.partial(attend_kernel, distances, joint, first, last),
        out_shape=out_shape,
        in_specs=[pl.BlockSpec(memory_space=pltpu.SMEM)]
        + whole(4 + len(blocks) + len(state)),
        out_specs=out_specs,
        scratch_shapes=scratch,
        compiler_params=params(10),
        cost_estimate=pl.CostEstimate(
            flops=800000000 * len(distances), bytes_accessed=3000000, transcendentals=1000000
        ),
        name="attend",
    )(where, query, position, start, offset, *blocks, *state)


def halves_kernel(keys_ref, values_ref, key_out, value_out):
    key_out[...] = keys_ref[:, 0:HD]
    value_out[...] = values_ref[:, HD : 2 * HD]


def take_halves(keys, values):
    return pl.pallas_call(
        halves_kernel,
        out_shape=[shape(BLOCK, HD)] * 2,
        in_specs=whole(2),
        out_specs=whole(2),
        compiler_params=params(4),
        name="take_halves",
    )(keys, values)


def share_and_attend(rows, make_query, tables, output_weight, core_weight, both_weight):
    tie = lax.optimization_barrier

    def onward(forward, backward):
        return move(forward, 1), move(backward, -1)

    one, back_one = onward(rows, rows)
    query = make_query()
    state = attend(tables, query, (0,), (1,), [rows], None, False)
    one, back_one, state = tie((one, back_one, state))
    two, back_two = onward(one, back_one)
    state = attend(tables, query, (1,), (1,), [one], state, False)
    two, back_two, state = tie((two, back_two, state))
    three, back_three = onward(two, back_two)
    state = attend(tables, query, (2, 6), (1, 1), [two, back_two], state, False)
    three, back_three, state, both_weight = tie((three, back_three, state, both_weight))
    y_weight = swap(both_weight, CC)
    key_half, value_half = take_halves(three, back_three)
    key_far = lax.ppermute(key_half, "ctx", [(3, 4), (4, 5), (5, 6)])
    value_far = lax.ppermute(value_half, "ctx", [(5, 4), (6, 5), (7, 6)])
    state = attend(tables, query, (3, 5), (1, 1), [three, back_three], state, False)
    key_far, value_far, state = tie((key_far, value_far, state))
    mine, to_y, to_core, to_both = attend(tables, query, (4,), (0, 2), [key_far, value_far], state, True)
    parts = [mine, swap(to_core, CC), swap(to_y, YY), swap(to_both, CC ^ YY)]
    return parts, [output_weight, core_weight, y_weight, both_weight]


HALF = D // 2
CHUNK = 384
X_ORDERS = ((XA, XB), (XB, XA))


def output_kernel(part, *refs):
    rows, weights, keeps, goes = refs[0:4], refs[4:8], refs[8], refs[9]
    for chunk in range(HALF // CHUNK):
        here = slice(part * HALF + chunk * CHUNK, part * HALF + (chunk + 1) * CHUNK)
        summed = jnp.zeros((128, CHUNK), jnp.float32)
        for row, weight in zip(rows, weights):
            group = jnp.dot(row[...], weight[:, here], preferred_element_type=jnp.float32)
            summed = summed + group.astype(jnp.bfloat16).astype(jnp.float32)
        summed = summed.astype(jnp.bfloat16)
        to = slice(chunk * CHUNK, (chunk + 1) * CHUNK)
        bit = BITS[X_ORDERS[part][0]]
        for place in range(4):
            out = goes if place & bit else keeps
            at = (place >> 1 if bit == 1 else place & 1) * ROWS
            out[at : at + ROWS, to] = summed[place * ROWS : (place + 1) * ROWS]


def project_out(part, rows, weights):
    return pl.pallas_call(
        functools.partial(output_kernel, part),
        out_shape=[shape(64, HALF)] * 2,
        in_specs=whole(8),
        out_specs=whole(2),
        compiler_params=params(16),
        cost_estimate=pl.CostEstimate(
            flops=2 * 128 * 1024 * HALF, bytes_accessed=6500000, transcendentals=0
        ),
        name="project_out",
    )(*rows, *weights)


def fold_kernel(*refs):
    kept, came, outs = refs[0:2], refs[2:4], refs[4:]
    for part in range(2):
        summed = (
            kept[part][...].astype(jnp.float32) + came[part][...].astype(jnp.float32)
        ).astype(jnp.bfloat16)
        outs[2 * part][...] = summed[0:ROWS]
        outs[2 * part + 1][...] = summed[ROWS : 2 * ROWS]


def fold(kept, came):
    return pl.pallas_call(
        fold_kernel,
        out_shape=[shape(ROWS, HALF)] * 4,
        in_specs=whole(4),
        out_specs=whole(4),
        compiler_params=params(8),
        name="fold_rows",
    )(*kept, *came)


def finish_kernel(residual_ref, gain_ref, *refs):
    kept, came, out, sums = refs[0:2], refs[2:4], refs[4], refs[5]
    square = jnp.zeros((ROWS, HD), jnp.float32)
    for part in range(2):
        for k in range(HALF // HD):
            here = slice(k * HD, (k + 1) * HD)
            summed = kept[part][:, here].astype(jnp.float32) + came[part][:, here].astype(
                jnp.float32
            )
            at = part * HALF + k * HD
            sums[:, at : at + HD] = summed
            square = square + summed * summed
    inverse = lax.rsqrt(jnp.sum(square, axis=-1, keepdims=True) / D + epsilon)
    for k in range(D // HD):
        here = slice(k * HD, (k + 1) * HD)
        out[:, here] = (
            residual_ref[:, here].astype(jnp.float32)
            + sums[:, here] * inverse * gain_ref[k : k + 1]
        ).astype(jnp.bfloat16)


def finish(residual, gain, kept, came):
    return pl.pallas_call(
        finish_kernel,
        out_shape=shape(ROWS, D),
        in_specs=whole(6),
        out_specs=whole(1)[0],
        scratch_shapes=[pltpu.VMEM((ROWS, D), jnp.float32)],
        compiler_params=params(6),
        name="finish",
    )(residual, gain.reshape(D // HD, HD), *kept, *came)


def reduce_tokens(rows, weights):
    kept, came = [], []
    for part in range(2):
        keeps, goes = project_out(part, rows, weights)
        kept.append(keeps)
        came.append(swap(goes, X_ORDERS[part][0]))
    halves = fold(kept, came)
    came = [swap(halves[2 * part + 1], X_ORDERS[part][1]) for part in range(2)]
    return halves[0::2], came


def body(
    residual_in,
    document_start,
    input_gain,
    query_weight,
    key_weight,
    value_weight,
    query_gain,
    key_gain,
    output_weight,
    post_gain,
):
    thirds = norm_rows(residual_in, input_gain)

    pieces, made, core_weight, both_weight = gather_tokens(
        thirds,
        document_start,
        swap(output_weight, CC),
        query_gain,
        key_gain,
        key_weight,
        value_weight,
    )
    cosine, sine, position, start, offset, query_gain, key_gain, pair_weight, where = made
    rows = project_key_value(pieces, pair_weight, key_gain, cosine, sine)
    parts, weights = share_and_attend(
        rows,
        lambda: project_query(pieces, query_weight, query_gain, cosine, sine),
        (where, position, start, offset),
        output_weight,
        core_weight,
        both_weight,
    )
    kept, came = reduce_tokens(parts, weights)
    return finish(residual_in, post_gain, kept, came)


def solution(mesh):
    return jax.shard_map(
        body,
        mesh=mesh,
        in_specs=(
            P(("docs", "ctx", "mp"), None),
            P(("docs", "ctx")),
            P(),
            P(None, "mp"),
            P(None, "mp"),
            P(None, "mp"),
            P(),
            P(),
            P("mp", None),
            P(),
        ),
        out_specs=P(("docs", "ctx", "mp"), None),
        check_vma=False,
    )
```

```python
import functools
import math

import jax
import jax.numpy as jnp
import numpy as np
from jax import lax
from jax.experimental import pallas as pl
from jax.experimental.pallas import tpu as pltpu
from jax.sharding import PartitionSpec as P

query_scalar = 168.0
rope_base = 1000000.0
rope_factor = 8.0
epsilon = 1e-06

D = 5376
THIRD = D // 3
HD = 128
ROWS = 32
BLOCK = 512

XA, XB, YY, CC = 2, 6, 8, 1
ORDERS = ((XA, XB, YY), (XB, YY, XA), (YY, XA, XB))
BITS = {XA: 1, XB: 2, YY: 4}


def mp_mask(index):
    return (XA if index & 1 else 0) ^ (XB if index & 2 else 0) ^ (YY if index & 4 else 0)


def gathered_order(part):
    first, second, third = (BITS[link] for link in ORDERS[part])
    return [
        (first if k & 1 else 0) | (second if k & 2 else 0) | (third if k & 4 else 0)
        for k in range(8)
    ]


def swap(value, link):
    return lax.ppermute(value, "mp", [(m, m ^ link) for m in range(16)])


def swap_y_both_ways(value):
    return lax.ppermute(
        value,
        ("docs", "mp"),
        [(d * 16 + m, (d ^ (m & 1)) * 16 + (m ^ YY)) for d in range(2) for m in range(16)],
    )


def whole(count):
    return [pl.BlockSpec(memory_space=pltpu.VMEM)] * count


def params(mebibytes):
    return pltpu.CompilerParams(vmem_limit_bytes=mebibytes * 1024 * 1024)


def shape(rows, columns, dtype=jnp.bfloat16):
    return jax.ShapeDtypeStruct((rows, columns), dtype)


def norm_kernel(x_hbm, gain_hbm, *refs):
    outs, x_ref, gain_ref, sem = refs[0:3], refs[3], refs[4], refs[5]
    copies = [
        pltpu.make_async_copy(x_hbm, x_ref, sem.at[0]),
        pltpu.make_async_copy(gain_hbm, gain_ref, sem.at[1]),
    ]
    for copy in copies:
        copy.start()
    for copy in copies:
        copy.wait()
    square = jnp.zeros((ROWS, HD), jnp.float32)
    for k in range(D // HD):
        x = x_ref[:, k * HD : (k + 1) * HD].astype(jnp.float32)
        square = square + x * x
    inverse = lax.rsqrt(jnp.sum(square, axis=-1, keepdims=True) / D + epsilon)
    for part, out in enumerate(outs):
        for k in range(THIRD // HD):
            at = part * (THIRD // HD) + k
            x = x_ref[:, at * HD : (at + 1) * HD].astype(jnp.float32)
            out[:, k * HD : (k + 1) * HD] = (x * inverse * gain_ref[at : at + 1]).astype(
                jnp.bfloat16
            )


def norm_rows(residual, gain):
    return pl.pallas_call(
        norm_kernel,
        out_shape=[shape(ROWS, THIRD)] * 3,
        in_specs=[pl.BlockSpec(memory_space=pltpu.HBM)] * 2,
        out_specs=whole(3),
        scratch_shapes=[
            pltpu.VMEM((ROWS, D), jnp.bfloat16),
            pltpu.VMEM((D // HD, HD), jnp.float32),
            pltpu.SemaphoreType.DMA((2,)),
        ],
        compiler_params=params(4),
        name="norm_rows",
    )(residual, gain.reshape(D // HD, HD))


def tables_kernel(
    starts_ref,
    first_ref,
    frequency_ref,
    query_gain_ref,
    key_gain_ref,
    key_weight_ref,
    value_weight_ref,
    cos_ref,
    sin_ref,
    position_ref,
    start_ref,
    offset_ref,
    query_gain_out,
    key_gain_out,
    weight_out,
    where_ref,
    natural,
    sem,
):
    copies = [
        pltpu.make_async_copy(source, weight_out.at[:, pl.ds(k * HD, HD)], sem.at[k])
        for k, source in enumerate((key_weight_ref, value_weight_ref))
    ]
    for copy in copies:
        copy.start()
    query_gain_out[...] = query_gain_ref[...]
    key_gain_out[...] = key_gain_ref[...]
    mine = lax.axis_index("mp")
    block = lax.axis_index("ctx")
    row = lax.broadcasted_iota(jnp.int32, (HD, HD), 0)
    lane = lax.broadcasted_iota(jnp.int32, (HD, HD), 1)
    for k in range(BLOCK // HD):
        spread = jnp.broadcast_to(starts_ref[k : k + 1].astype(jnp.float32), (HD, HD))
        column = jnp.sum(jnp.where(row == lane, spread, 0.0), axis=-1, keepdims=True)
        natural[k * HD : (k + 1) * HD] = jnp.broadcast_to(column, (HD, HD)).astype(jnp.int32)
    inner = lax.broadcasted_iota(jnp.int32, (ROWS, HD), 0)
    along = lax.broadcasted_iota(jnp.int32, (1, BLOCK), 1)
    offset = along
    sign = jnp.where(
        lax.broadcasted_iota(jnp.int32, (ROWS, HD), 1) < HD // 2, -1.0, 1.0
    )
    for k in range(16):
        owner = mine ^ (mp_mask(k & 7) ^ (k >> 3))
        here = slice(k * ROWS, (k + 1) * ROWS)
        start = natural[pl.ds(pl.multiple_of(owner * ROWS, ROWS), ROWS)]
        position = inner + (block * BLOCK + owner * ROWS)
        start_ref[here] = start
        position_ref[here] = position
        angles = ((position - start).astype(jnp.float32) / rope_factor) * frequency_ref[...]
        cos_ref[here] = jnp.cos(angles)
        sin_ref[here] = jnp.sin(angles) * sign
        inside = (along >= k * ROWS) & (along < (k + 1) * ROWS)
        offset = jnp.where(inside, along + (owner - k) * ROWS, offset)
    offset_ref[...] = offset
    where_ref[0] = block
    where_ref[1] = block - (first_ref[0] >> 9) + 1
    where_ref[2] = first_ref[BLOCK - 1]
    for copy in copies:
        copy.wait()


def make_tables(document_start, query_gain, key_gain, key_weight, value_weight):
    frequency = np.float32(rope_base) ** (
        -(np.arange(HD // 2, dtype=np.float32) * np.float32(2.0) / np.float32(HD))
    )
    frequency = jnp.asarray(np.concatenate([frequency, frequency])[None, :], jnp.float32)
    wide = lambda kind: jax.ShapeDtypeStruct((BLOCK, HD), kind)
    return pl.pallas_call(
        tables_kernel,
        out_shape=[
            wide(jnp.float32),
            wide(jnp.float32),
            wide(jnp.int32),
            wide(jnp.int32),
            jax.ShapeDtypeStruct((1, BLOCK), jnp.int32),
            shape(1, HD, jnp.float32),
            shape(1, HD, jnp.float32),
            shape(D, 2 * HD),
            jax.ShapeDtypeStruct((3,), jnp.int32),
        ],
        in_specs=[
            pl.BlockSpec(memory_space=pltpu.VMEM),
            pl.BlockSpec(memory_space=pltpu.SMEM),
            *whole(3),
            pl.BlockSpec(memory_space=pltpu.HBM),
            pl.BlockSpec(memory_space=pltpu.HBM),
        ],
        out_specs=whole(8) + [pl.BlockSpec(memory_space=pltpu.SMEM)],
        scratch_shapes=[pltpu.VMEM((BLOCK, HD), jnp.int32), pltpu.SemaphoreType.DMA((2,))],
        compiler_params=params(7),
        cost_estimate=pl.CostEstimate(
            flops=4000000, bytes_accessed=1000000, transcendentals=131072
        ),
        name="tables",
    )(
        document_start.reshape(BLOCK // HD, HD),
        document_start,
        frequency,
        query_gain.reshape(1, HD),
        key_gain.reshape(1, HD),
        key_weight,
        value_weight,
    )


def join_kernel(extra, *refs):
    held, came, outs = refs[0:3], refs[3:6], refs[6:]
    for part in range(3):
        rows = held[part].shape[0]
        outs[part][0:rows] = held[part][...]
        outs[part][rows : 2 * rows] = came[part][...]
        if extra:
            outs[3][part, 0:rows] = held[part][...]
            outs[3][part, rows : 2 * rows] = came[part][...]


def join(held, came, extra):
    rows = held[0].shape[0]
    outs = [shape(2 * rows, THIRD)] * 3
    if extra:
        outs = outs + [jax.ShapeDtypeStruct((3, 2 * rows, THIRD), jnp.bfloat16)]
    return pl.pallas_call(
        functools.partial(join_kernel, extra),
        out_shape=outs,
        in_specs=whole(6),
        out_specs=whole(len(outs)),
        compiler_params=params(10),
        name="join_rows",
    )(*held, *came)


def gather_tokens(thirds, document_start, core_weight, *small):
    came = [swap(thirds[p], ORDERS[p][0]) for p in range(3)]
    two = join(thirds, came, False)
    came = [swap(two[p], ORDERS[p][1]) for p in range(3)]
    *came, document_start, core_weight = lax.optimization_barrier(
        (*came, document_start, core_weight)
    )
    *four, packed = join(two, came, True)
    late = [swap(four[p], ORDERS[p][2]) for p in range(3)]
    other = swap(packed, CC)
    tables = make_tables(document_start, *small)
    other_late = [swap(late[p], CC) for p in range(3)]
    held = lax.optimization_barrier((*late, *tables, core_weight, other))
    late, tables, core_weight, other = held[0:3], held[3:12], held[12], held[13]
    both_weight = swap_y_both_ways(core_weight)
    return (four, late, other, other_late), tables, core_weight, both_weight


def rotate(raw, gain, cosine, sine):
    inverse = lax.rsqrt(jnp.mean(raw * raw, axis=-1, keepdims=True) + epsilon)
    scaled = raw * inverse * gain
    turned = pltpu.roll(scaled, HD // 2, 1)
    return (scaled * cosine + turned * sine).astype(jnp.bfloat16)


def projected(x_refs, w_ref, cores):
    four, late = x_refs[0:3], x_refs[3:6]
    if 1 in cores:
        other, other_late = x_refs[6], x_refs[7:10]
    total = None
    for part in range(3):
        order = gathered_order(part)
        rows = []
        for core in cores:
            for place in range(8):
                k = order.index(place)
                at = (k % 4) * ROWS
                if core == 0:
                    rows.append((four if k < 4 else late)[part][at : at + ROWS])
                elif k < 4:
                    rows.append(other[part, at : at + ROWS])
                else:
                    rows.append(other_late[part][at : at + ROWS])
        product = jnp.dot(
            jnp.concatenate(rows, axis=0),
            w_ref[part * THIRD : (part + 1) * THIRD],
            preferred_element_type=jnp.float32,
        )
        total = product if part == 0 else total + product
    return total


def query_kernel(*refs):
    w_ref, gain_ref, cos_ref, sin_ref, out_ref = refs[10:]
    total = projected(refs[0:10], w_ref, (0, 1))
    gain = gain_ref[...]
    for head in range(2):
        here = slice(head * HD, (head + 1) * HD)
        out_ref[:, here] = rotate(total[:, here], gain, cos_ref[...], sin_ref[...])


def key_value_kernel(core, *refs):
    count = 10 if core else 6
    w_ref, gain_ref, cos_ref, sin_ref = refs[count : count + 4]
    out_ref = refs[-1]
    total = projected(refs[0:count], w_ref, (core,))
    table = slice(core * 256, (core + 1) * 256)
    here = table if core else slice(0, 256)
    if core:
        out_ref[0:256] = refs[count + 4][...]
    out_ref[here, 0:HD] = rotate(
        total[:, 0:HD], gain_ref[...], cos_ref[table], sin_ref[table]
    )
    out_ref[here, HD : 2 * HD] = total[:, HD : 2 * HD].astype(jnp.bfloat16)


def project_call(kernel, rows, flops, name, *operands):
    return pl.pallas_call(
        kernel,
        out_shape=shape(rows, 2 * HD),
        in_specs=whole(len(operands)),
        out_specs=whole(1)[0],
        compiler_params=params(14),
        cost_estimate=pl.CostEstimate(flops=flops, bytes_accessed=9000000, transcendentals=0),
        name=name,
    )(*operands)


def project_query(pieces, weight, gain, cosine, sine):
    four, late, other, other_late = pieces
    flops = 2 * BLOCK * D * 2 * HD
    return project_call(
        query_kernel, BLOCK, flops, "project_q",
        *four, *late, other, *other_late, weight, gain, cosine, sine,
    )


def project_key_value(pieces, weight, gain, cosine, sine):
    four, late, other, other_late = pieces
    flops = BLOCK * D * 2 * HD
    mine = project_call(
        functools.partial(key_value_kernel, 0), 256, flops, "project_kv_mine",
        *four, *late, weight, gain, cosine, sine,
    )
    return project_call(
        functools.partial(key_value_kernel, 1), BLOCK, flops, "project_kv",
        *four, *late, other, *other_late, weight, gain, cosine, sine, mine,
    )


NEG = -1e30
TILE = 256


def move(value, step):
    return lax.ppermute(value, "ctx", [(c, (c + step) % 8) for c in range(8)])


def attend_kernel(distances, joint, first, last, *refs):
    where_ref, q_ref, position_ref, start_ref, offset_ref = refs[0:5]
    refs = refs[5:]
    blocks, refs = refs[: len(joint)], refs[len(joint) :]
    if not first:
        old_state, refs = refs[0:3], refs[3:]
    if last:
        out_refs, state = refs[0:4], refs[4:7]
    else:
        state = refs[0:3]
    top, total, acc = state
    block = where_ref[0]
    live = where_ref[1]
    rows_here = q_ref.shape[0]
    factor = math.log2(math.e) / math.sqrt(query_scalar)

    def step(distance, keys_ref, values_ref, source, masked=True):
        opening = source is None
        keys = keys_ref[...]
        values = values_ref[...]
        key_index = offset_ref[...] + (block - distance) * BLOCK
        for tile in range(rows_here // TILE):
            rows = slice(tile * TILE, (tile + 1) * TILE)
            position = position_ref[rows]
            start = start_ref[rows]
            for head in range(2):
                scores = lax.dot_general(
                    q_ref[rows, head * HD : (head + 1) * HD],
                    keys,
                    (((1,), (1,)), ((), ())),
                    preferred_element_type=jnp.float32,
                )
                pieces = []
                for k in range(BLOCK // HD):
                    index = key_index[:, k * HD : (k + 1) * HD]
                    allowed = index >= start
                    if distance == 0:
                        allowed = allowed & (index <= position)
                    piece = scores[:, k * HD : (k + 1) * HD] * factor
                    pieces.append(jnp.where(allowed, piece, NEG) if masked else piece)
                best = jnp.maximum(
                    jnp.maximum(pieces[0], pieces[1]), jnp.maximum(pieces[2], pieces[3])
                )
                best = jnp.max(best, axis=-1, keepdims=True)
                if opening:
                    new = jnp.broadcast_to(best, (TILE, HD))
                else:
                    old = source[0][head, rows]
                    new = jnp.maximum(old, best)
                exps = [jnp.exp2(piece - new) for piece in pieces]
                sums = (exps[0] + exps[1]) + (exps[2] + exps[3])
                weights = jnp.concatenate([e.astype(jnp.bfloat16) for e in exps], axis=1)
                product = jnp.dot(weights, values, preferred_element_type=jnp.float32)
                if not opening:
                    fade = jnp.exp2(old - new)
                    sums = source[1][head, rows] * fade + sums
                    product = source[2][head, rows] * fade + product
                total[head, rows] = sums
                acc[head, rows] = product
                top[head, rows] = new

    def keep():
        for new_ref, old_ref in zip(state, old_state):
            new_ref[...] = old_ref[...]

    source = None if first else old_state
    k = 0
    for distance, whole_block in zip(distances, joint):
        if whole_block:
            keys_ref = blocks[k].at[:, pl.ds(0, HD)]
            values_ref = blocks[k].at[:, pl.ds(HD, HD)]
            k += 1
        else:
            keys_ref, values_ref = blocks[k], blocks[k + 1]
            k += 2
        if distance == 0:
            step(0, keys_ref, values_ref, None)
        else:
            is_live = distance < live
            is_whole = where_ref[2] <= (block - distance) * BLOCK
            for masked in (False, True):
                pl.when(is_live & (is_whole != masked))(
                    functools.partial(step, distance, keys_ref, values_ref, source, masked)
                )
            if source is not state:
                pl.when(distance >= live)(keep)
        source = state
    if last:
        for head in range(2):
            for quarter in range(4):
                here = slice(quarter * 128, (quarter + 1) * 128)
                denominator = jnp.sum(total[head, here], axis=-1, keepdims=True)
                out_refs[quarter][:, head * HD : (head + 1) * HD] = (
                    acc[head, here] / denominator
                ).astype(jnp.bfloat16)


def attend(tables, query, distances, joint, blocks, state, last):
    where, position, start, offset = tables
    first = state is None
    state = () if first else tuple(state)
    state_shape = jax.ShapeDtypeStruct((2, BLOCK, HD), jnp.float32)
    if last:
        out_shape, out_specs = [shape(128, 2 * HD)] * 4, whole(4)
        scratch = [pltpu.VMEM((2, BLOCK, HD), jnp.float32)] * 3
    else:
        out_shape, out_specs = [state_shape] * 3, whole(3)
        scratch = []
    return pl.pallas_call(
        functools.partial(attend_kernel, distances, joint, first, last),
        out_shape=out_shape,
        in_specs=[pl.BlockSpec(memory_space=pltpu.SMEM)]
        + whole(4 + len(blocks) + len(state)),
        out_specs=out_specs,
        scratch_shapes=scratch,
        compiler_params=params(10),
        cost_estimate=pl.CostEstimate(
            flops=800000000 * len(distances), bytes_accessed=3000000, transcendentals=1000000
        ),
        name="attend",
    )(where, query, position, start, offset, *blocks, *state)


def halves_kernel(keys_ref, values_ref, key_out, value_out):
    key_out[...] = keys_ref[:, 0:HD]
    value_out[...] = values_ref[:, HD : 2 * HD]


def take_halves(keys, values):
    return pl.pallas_call(
        halves_kernel,
        out_shape=[shape(BLOCK, HD)] * 2,
        in_specs=whole(2),
        out_specs=whole(2),
        compiler_params=params(4),
        name="take_halves",
    )(keys, values)


def share_and_attend(rows, make_query, tables, output_weight, core_weight, both_weight):
    tie = lax.optimization_barrier

    def onward(forward, backward):
        return move(forward, 1), move(backward, -1)

    one, back_one = onward(rows, rows)
    query = make_query()
    state = attend(tables, query, (0,), (1,), [rows], None, False)
    one, back_one, state = tie((one, back_one, state))
    two, back_two = onward(one, back_one)
    state = attend(tables, query, (1,), (1,), [one], state, False)
    two, back_two, state = tie((two, back_two, state))
    three, back_three = onward(two, back_two)
    state = attend(tables, query, (2, 6), (1, 1), [two, back_two], state, False)
    three, back_three, state, both_weight = tie((three, back_three, state, both_weight))
    y_weight = swap(both_weight, CC)
    key_half, value_half = take_halves(three, back_three)
    key_far = lax.ppermute(key_half, "ctx", [(3, 4), (4, 5), (5, 6)])
    value_far = lax.ppermute(value_half, "ctx", [(5, 4), (6, 5), (7, 6)])
    state = attend(tables, query, (3, 5), (1, 1), [three, back_three], state, False)
    key_far, value_far, state = tie((key_far, value_far, state))
    mine, to_y, to_core, to_both = attend(tables, query, (4,), (0, 2), [key_far, value_far], state, True)
    parts = [mine, swap(to_core, CC), swap(to_y, YY), swap(to_both, CC ^ YY)]
    return parts, [output_weight, core_weight, y_weight, both_weight]


HALF = D // 2
CHUNK = 384
X_ORDERS = ((XA, XB), (XB, XA))


def output_kernel(part, *refs):
    rows, weights, keeps, goes = refs[0:4], refs[4:8], refs[8], refs[9]
    for chunk in range(HALF // CHUNK):
        here = slice(part * HALF + chunk * CHUNK, part * HALF + (chunk + 1) * CHUNK)
        summed = jnp.zeros((128, CHUNK), jnp.float32)
        for row, weight in zip(rows, weights):
            group = jnp.dot(row[...], weight[:, here], preferred_element_type=jnp.float32)
            summed = summed + group.astype(jnp.bfloat16).astype(jnp.float32)
        summed = summed.astype(jnp.bfloat16)
        to = slice(chunk * CHUNK, (chunk + 1) * CHUNK)
        bit = BITS[X_ORDERS[part][0]]
        for place in range(4):
            out = goes if place & bit else keeps
            at = (place >> 1 if bit == 1 else place & 1) * ROWS
            out[at : at + ROWS, to] = summed[place * ROWS : (place + 1) * ROWS]


def project_out(part, rows, weights):
    return pl.pallas_call(
        functools.partial(output_kernel, part),
        out_shape=[shape(64, HALF)] * 2,
        in_specs=whole(8),
        out_specs=whole(2),
        compiler_params=params(16),
        cost_estimate=pl.CostEstimate(
            flops=2 * 128 * 1024 * HALF, bytes_accessed=6500000, transcendentals=0
        ),
        name="project_out",
    )(*rows, *weights)


def fold_kernel(*refs):
    kept, came, outs = refs[0:2], refs[2:4], refs[4:]
    for part in range(2):
        summed = (
            kept[part][...].astype(jnp.float32) + came[part][...].astype(jnp.float32)
        ).astype(jnp.bfloat16)
        outs[2 * part][...] = summed[0:ROWS]
        outs[2 * part + 1][...] = summed[ROWS : 2 * ROWS]


def fold(kept, came):
    return pl.pallas_call(
        fold_kernel,
        out_shape=[shape(ROWS, HALF)] * 4,
        in_specs=whole(4),
        out_specs=whole(4),
        compiler_params=params(8),
        name="fold_rows",
    )(*kept, *came)


def finish_kernel(residual_ref, gain_ref, *refs):
    kept, came, out, sums = refs[0:2], refs[2:4], refs[4], refs[5]
    square = jnp.zeros((ROWS, HD), jnp.float32)
    for part in range(2):
        for k in range(HALF // HD):
            here = slice(k * HD, (k + 1) * HD)
            summed = kept[part][:, here].astype(jnp.float32) + came[part][:, here].astype(
                jnp.float32
            )
            at = part * HALF + k * HD
            sums[:, at : at + HD] = summed
            square = square + summed * summed
    inverse = lax.rsqrt(jnp.sum(square, axis=-1, keepdims=True) / D + epsilon)
    for k in range(D // HD):
        here = slice(k * HD, (k + 1) * HD)
        out[:, here] = (
            residual_ref[:, here].astype(jnp.float32)
            + sums[:, here] * inverse * gain_ref[k : k + 1]
        ).astype(jnp.bfloat16)


def finish(residual, gain, kept, came):
    return pl.pallas_call(
        finish_kernel,
        out_shape=shape(ROWS, D),
        in_specs=whole(6),
        out_specs=whole(1)[0],
        scratch_shapes=[pltpu.VMEM((ROWS, D), jnp.float32)],
        compiler_params=params(6),
        name="finish",
    )(residual, gain.reshape(D // HD, HD), *kept, *came)


def reduce_tokens(rows, weights):
    kept, came = [], []
    for part in range(2):
        keeps, goes = project_out(part, rows, weights)
        kept.append(keeps)
        came.append(swap(goes, X_ORDERS[part][0]))
    halves = fold(kept, came)
    came = [swap(halves[2 * part + 1], X_ORDERS[part][1]) for part in range(2)]
    return halves[0::2], came


def body(
    residual_in,
    document_start,
    input_gain,
    query_weight,
    key_weight,
    value_weight,
    query_gain,
    key_gain,
    output_weight,
    post_gain,
):
    thirds = norm_rows(residual_in, input_gain)

    pieces, made, core_weight, both_weight = gather_tokens(
        thirds,
        document_start,
        swap(output_weight, CC),
        query_gain,
        key_gain,
        key_weight,
        value_weight,
    )
    cosine, sine, position, start, offset, query_gain, key_gain, pair_weight, where = made
    rows = project_key_value(pieces, pair_weight, key_gain, cosine, sine)
    parts, weights = share_and_attend(
        rows,
        lambda: project_query(pieces, query_weight, query_gain, cosine, sine),
        (where, position, start, offset),
        output_weight,
        core_weight,
        both_weight,
    )
    kept, came = reduce_tokens(parts, weights)
    return finish(residual_in, post_gain, kept, came)


def solution(mesh):
    return jax.shard_map(
        body,
        mesh=mesh,
        in_specs=(
            P(("docs", "ctx", "mp"), None),
            P(("docs", "ctx")),
            P(),
            P(None, "mp"),
            P(None, "mp"),
            P(None, "mp"),
            P(),
            P(),
            P("mp", None),
            P(),
        ),
        out_specs=P(("docs", "ctx", "mp"), None),
        check_vma=False,
    )
```
